256 devices in a mesh: sub: 64 (over y, z, core), crs: 4 (over x).
Axes of the slice: x: 4, y: 4, z: 8, core: 2. Of those that a mesh axis runs over, the one named last changes fastest.
Arguments:
- loads: float32 [4096, 128, 128], P(('sub', 'crs')), may hold values from -6 to 6
- stiffness: float32 [4096, 6, 128, 128], P(('sub', 'crs'))
- inv_diag: float32 [4096, 128, 128], P(('sub', 'crs'))
- columns: int32 [4096, 6], P(('sub', 'crs')), may hold values from 0 to 17, as said below
- send_lists: int32 [256, 2, 1], P(('sub', 'crs')), may hold values from 0 to 15
- restrict_weights: float32 [4096, 128], P(('sub', 'crs')), may hold values from -4 to 4
- coarse_map: int32 [4096], P(('sub', 'crs')), may hold values from 0 to 2047
- coarse_diag: float32 [16, 128], replicated, may hold values from 0.5 to 2
Outputs:
- solution: float32 [4096, 128, 128], P(('sub', 'crs'))
- residual: float32 [4096, 128, 128], P(('sub', 'crs'))
- precond_residual: float32 [4096, 128, 128], P(('sub', 'crs'))
The draws below stay inside these ranges and needn't reach their ends.
Inputs may be any that keep to these rules, and one draw needn't show every extreme that they name: `columns`: entry 0 of every block row is the block's own position in its subdomain, i % 16; the other entries index the extended list.
All inputs are finite; a program needn't handle non-finite values.
Results may differ from the reference program's by a relative error of at most 0.0003.
Values sent between devices are 32-bit elements; how exact they have to be, the bound alone decides.
No kernel may reach another device: no remote copies, remote signals or barrier semaphores. Data moves between devices by JAX's collectives and lax.ppermute only.
A program may use at most 64 MiB of HBM per device.

```python
import jax
import jax.numpy as jnp
from jax import lax

NB = 16
BLK = 128
KB = 6
G = 1
NRHS = 128
CCOLS = 128
SWEEPS = 4
ITERS = 2
BLOCKS = 4096
CROWS = 16
CELLS = 2048
N_SUB = 64
N_CRS = 4


def draw_stiffness(key, part):
    key = jax.random.fold_in(key, 11)
    shape = (BLOCKS, KB, BLK, BLK)
    noise = jax.random.normal(key, shape, jnp.float32)
    eye = (jnp.arange(BLK)[:, None] == jnp.arange(BLK)[None, :]).astype(jnp.float32)
    first = (jnp.arange(KB) == 0).astype(jnp.float32)[None, :, None, None]
    scale = jnp.where(first > 0.5, 0.3, 0.35) / jnp.sqrt(jnp.float32(BLK))
    return noise * scale + 4.0 * first * eye[None, None]


def draw_inv_diag(key, part):
    key = jax.random.fold_in(key, 23)
    shape = (BLOCKS, BLK, BLK)
    noise = jax.random.normal(key, shape, jnp.float32)
    eye = (jnp.arange(BLK)[:, None] == jnp.arange(BLK)[None, :]).astype(jnp.float32)
    return 0.25 * eye[None] + noise * (0.08 / jnp.sqrt(jnp.float32(BLK)))


def draw_columns(key, part):
    key = jax.random.fold_in(key, 37)
    others = jax.random.randint(key, (BLOCKS, KB), 0, NB + 2 * G, jnp.int32)
    own = (jnp.arange(BLOCKS, dtype=jnp.int32) % NB)[:, None]
    first = (jnp.arange(KB, dtype=jnp.int32) == 0)[None, :]
    return jnp.where(first, own, others).astype(jnp.int32)


def place_ends(drawn, own_key, low, high):
    longest = drawn.shape.index(max(drawn.shape))
    spots = []
    for shift in (0, 1):
        where = [jax.random.randint(jax.random.fold_in(own_key, axis), (), 0, length) for axis, length in enumerate(drawn.shape)]
        where[longest] = (where[longest] + shift) % drawn.shape[longest]
        spots.append(tuple(where))
    return drawn.at[spots[0]].set(low).at[spots[1]].set(high)


def shard_levels(key, shape, pieces, least, top_value):
    loudness = 1.0
    for dim, blocks in pieces:
        heights = jax.random.uniform(jax.random.fold_in(jax.random.fold_in(key, 6), dim), (blocks,), jnp.float32, least / len(pieces), top_value / len(pieces))
        loudness = loudness * jnp.repeat(jnp.exp(heights), shape[dim] // blocks).reshape((-1,) + (1,) * (len(shape) - 1 - dim))
    return loudness


def normal_values(key, shape, scale, most, cuts=(), kind=jnp.bfloat16):
    array = jax.random.normal(key, shape, jnp.float32) * scale
    if len(cuts) > 0:
        array = shard_levels(key, shape, cuts, -0.22, 0.18) * array
    return jnp.clip(array, min=-most, max=most).astype(kind)


def setup_inputs(seed: int = 0) -> dict:
    keys = jax.random.split(jax.random.key(seed), 9)
    return {
        "loads": normal_values(keys[0], (BLOCKS, BLK, NRHS), 1.0, 6.0, ((0, 256),), jnp.float32),
        "stiffness": draw_stiffness(jax.random.fold_in(keys[8], 71), 0),
        "inv_diag": draw_inv_diag(jax.random.fold_in(keys[8], 71), 0),
        "columns": draw_columns(jax.random.fold_in(keys[8], 71), 0),
        "send_lists": place_ends(jax.random.randint(keys[4], (N_SUB * N_CRS, 2, G), 0, NB), jax.random.fold_in(keys[4], 1), 0, NB - 1).astype(jnp.int32),
        "restrict_weights": normal_values(keys[5], (BLOCKS, BLK), 0.25, 4.0, ((0, 256),), jnp.float32),
        "coarse_map": place_ends(jax.random.randint(keys[6], (BLOCKS,), 0, CELLS), jax.random.fold_in(keys[6], 1), 0, CELLS - 1).astype(jnp.int32),
        "coarse_diag": jnp.clip(jax.random.uniform(keys[7], (CROWS, CCOLS), jnp.float32, 0.5, 2.0), 0.5, 2.0),
    }


OMEGA = 0.8
HIGH = lax.Precision.HIGHEST


def extended_list(field, send_lists):
    devices = N_SUB * N_CRS
    split = field.reshape(devices, NB, BLK, NRHS)
    idx = send_lists.reshape(devices, 2 * G)
    packed = jax.vmap(lambda blocks, chosen: jnp.take(blocks, chosen, axis=0))(split, idx)
    lower = jnp.roll(packed[:, G:], 1, axis=0)
    upper = jnp.roll(packed[:, :G], -1, axis=0)
    return jnp.concatenate([split, lower, upper], axis=1)


def operator(field, stiffness, columns, send_lists):
    devices = N_SUB * N_CRS
    extended = extended_list(field, send_lists)

    def one_domain(items):
        ext, mats, cols = items
        picked = jnp.take(ext, cols, axis=0)
        return jnp.einsum('bkij,bkjr->bir', mats, picked, precision=HIGH, preferred_element_type=jnp.float32)

    result = lax.map(one_domain, (extended, stiffness.reshape(devices, NB, KB, BLK, BLK), columns.reshape(devices, NB, KB)))
    return result.reshape(BLOCKS, BLK, NRHS)


def coarse_apply(field, diag_full):
    rows = jnp.pad(field, ((1, 1), (0, 0), (0, 0)))
    cols = jnp.pad(field, ((0, 0), (1, 1), (0, 0)))
    beside = rows[2:] + rows[:-2] + cols[:, 2:] + cols[:, :-2]
    return diag_full * field - beside


def precondition(field, inv_diag, restrict_weights, coarse_map, coarse_diag):
    local = jnp.einsum('bij,bjr->bir', inv_diag, field, precision=HIGH, preferred_element_type=jnp.float32)
    reduced = jnp.einsum('bi,bir->br', restrict_weights, field, precision=HIGH, preferred_element_type=jnp.float32)
    coarse_rhs = jax.ops.segment_sum(reduced, coarse_map, CELLS).reshape(CROWS, CCOLS, NRHS)
    diag_full = (4.0 + coarse_diag)[:, :, None]
    coarse = jnp.zeros_like(coarse_rhs)
    for sweep in range(SWEEPS):
        coarse = coarse + OMEGA * (coarse_rhs - coarse_apply(coarse, diag_full)) / diag_full
    picked = jnp.take(coarse.reshape(CELLS, NRHS), coarse_map, axis=0)
    return local + restrict_weights[:, :, None] * picked[:, None, :]


def reference(loads, stiffness, inv_diag, columns, send_lists, restrict_weights, coarse_map, coarse_diag):
    solution = jnp.zeros_like(loads)
    residual = loads
    precond = precondition(residual, inv_diag, restrict_weights, coarse_map, coarse_diag)
    direction = precond
    gamma = jnp.sum(residual * precond, axis=(0, 1))
    for step in range(ITERS):
        image = operator(direction, stiffness, columns, send_lists)
        alpha = gamma / jnp.sum(direction * image, axis=(0, 1))
        solution = solution + alpha * direction
        residual = residual - alpha * image
        precond = precondition(residual, inv_diag, restrict_weights, coarse_map, coarse_diag)
        gamma_next = jnp.sum(residual * precond, axis=(0, 1))
        direction = precond + (gamma_next / gamma) * direction
        gamma = gamma_next
    return solution, residual, precond
```

```python
import functools

import jax
import jax.numpy as jnp
from jax import lax
from jax.experimental import pallas as pl
from jax.experimental.pallas import tpu as pltpu
from jax.sharding import Mesh, PartitionSpec as P

OMEGA = 0.8
SWEEPS = 4
NB = 16
BLK = 128
KB = 6
EXT = 18
ROWS = 24
CROWS = 16
RING = ("y", "z", "core", "crs")
GATHER = ("y", "z")
SCATTER = ("core", "crs")
F32 = jnp.float32
BF16 = jnp.bfloat16
VMEM = 48 * 1024 * 1024


def sweep_coefficients():
    total = [0.0] * SWEEPS
    power = [1.0]
    for _ in range(SWEEPS):
        for i, c in enumerate(power):
            total[i] += c
        grown = [0.0] * (len(power) + 1)
        for i, c in enumerate(power):
            grown[i] += c * (1.0 - OMEGA)
            grown[i + 1] += c * OMEGA
        power = grown
    return total


def split(x):
    high = x.astype(BF16)
    return high, (x - high.astype(F32)).astype(BF16)


def dot(a, b):
    return jnp.dot(a, b, preferred_element_type=F32)


def dot3(a, b):
    ah, al = split(a)
    bh, bl = split(b)
    return dot(ah, bh) + (dot(ah, bl) + dot(al, bh))


def call(kernel, outs, *, scratch=(), specs=None, flops=0, moved=0):
    return pl.pallas_call(
        kernel,
        out_shape=[jax.ShapeDtypeStruct(s, d) for s, d in outs],
        in_specs=specs,
        scratch_shapes=list(scratch),
        compiler_params=pltpu.CompilerParams(vmem_limit_bytes=VMEM),
        cost_estimate=pl.CostEstimate(flops=flops, bytes_accessed=moved, transcendentals=0),
    )


def restrict_kernel(r_ref, w_ref, cells_ref, msg_ref):
    wt = w_ref[...].T
    rows = [jnp.sum(wt[:, i : i + 1] * r_ref[i], axis=0, keepdims=True) for i in range(NB)]
    rows = jnp.concatenate(rows + [cells_ref[...]], axis=0)
    for a in range(msg_ref.shape[0]):
        msg_ref[a] = rows


def local_kernel(send_ref, f_ref, d_ref, w_ref, info_ref, out_ref, prev_ref, next_ref):
    for i in range(NB):
        out_ref[i] = dot3(d_ref[i], f_ref[i])
    for slot, ref in ((0, prev_ref), (1, next_ref)):
        ref[:BLK] = out_ref[send_ref[0, slot]]
        ref[BLK:] = info_ref[slot]


def sweep_kernel(t_ref, diag_ref, out_ref):
    inv = 1.0 / (4.0 + diag_ref[...])
    coef = sweep_coefficients()
    lane = lax.broadcasted_iota(jnp.int32, (8, BLK), 1)

    def chunk(c, _):
        cell = t_ref[pl.ds(pl.multiple_of(c * 8, 8), 8), :]
        spot = [cell == (lane + BLK * r).astype(F32) for r in range(CROWS)]
        t = [jnp.where(spot[r], coef[-1], 0.0) for r in range(CROWS)]
        for power in range(SWEEPS - 2, -1, -1):
            y = [t[r] * inv[r : r + 1] for r in range(CROWS)]
            new = []
            for r in range(CROWS):
                v = jnp.where(lane == 0, 0.0, pltpu.roll(y[r], 1, 1))
                v = v + jnp.where(lane == BLK - 1, 0.0, pltpu.roll(y[r], BLK - 1, 1))
                if r > 0:
                    v = v + y[r - 1]
                if r < CROWS - 1:
                    v = v + y[r + 1]
                new.append(v + jnp.where(spot[r], coef[power], 0.0))
            t = new
        for r in range(CROWS):
            out_ref[r, pl.ds(pl.multiple_of(c * 8, 8), 8), :] = t[r] * (inv[r : r + 1] * OMEGA)
        return 0

    lax.fori_loop(0, t_ref.shape[0] // 8, chunk, 0)


def coarse_kernel(rows_ref, g_ref, part_ref, wh_ref, wl_ref, sh_ref, sl_ref, oh_ref):
    devs = g_ref.shape[0]
    sources = devs * NB
    targets = rows_ref.shape[1]
    cells = g_ref[:, NB : NB + 1, :].reshape(devs, BLK)
    cells = jnp.sum(cells.reshape(devs // 8, 8, BLK), axis=1)
    sub = lax.broadcasted_iota(jnp.int32, (BLK, BLK), 0)
    for r in range(CROWS):
        here = slice(r * BLK, (r + 1) * BLK)
        high, low = split(rows_ref[r])
        sh_ref[:, here] = high
        sl_ref[:, here] = low
        index = (sub + r * BLK).astype(F32)
        for q in range(devs // 8):
            hit = jnp.where(cells[q : q + 1] == index, 1.0, 0.0)
            oh_ref[here, q * BLK : (q + 1) * BLK] = hit.astype(BF16)
    w = dot(sh_ref[...], oh_ref[...]) + dot(sl_ref[...], oh_ref[...])
    wh, wl = split(w)
    wh_ref[...] = wh
    wl_ref[...] = wl
    gh, gl = split(g_ref[:, :NB, :].reshape(sources, BLK))
    part = dot(wh, gh) + (dot(wh, gl) + dot(wl, gh))
    part_ref[...] = part.reshape(part_ref.shape)


def apply_kernel(wh_ref, wl_ref, g_ref, part_ref):
    devs = g_ref.shape[0]
    gh, gl = split(g_ref[:, :NB, :].reshape(devs * NB, BLK))
    wh = wh_ref[...]
    part = dot(wh, gh) + (dot(wh, gl) + dot(wl_ref[...], gh))
    part = part.reshape(part_ref.shape)
    part_ref[:, :NB, :] = part[:, :NB, :]
    sums = jnp.sum(g_ref[:, NB:, :], axis=0)
    part_ref[:, NB:, :] = part[:, NB:, :] + sums[None]


def operator_kernel(first, cols_ref, s_ref, f_ref, lo_ref, up_ref, *rest):
    if first:
        w_ref, out_ref, q_ref, xh, xl = rest
    else:
        out_ref, xh, xl = rest
    step = pl.program_id(0)
    per = s_ref.shape[0]

    @pl.when(step == 0)
    def _():
        if first:
            wt = w_ref[...].T
            lane = lax.broadcasted_iota(jnp.int32, (BLK, BLK), 1)
            turned = jnp.concatenate(
                [lo_ref[BLK:, :], up_ref[BLK:, :]], axis=0
            ).T
        for e in range(EXT):
            x = f_ref[e] if e < NB else (lo_ref, up_ref)[e - NB][:BLK, :]
            high, low = split(x)
            xh[e, :, :BLK] = high
            xl[e, :, :BLK] = low
            if first:
                col = wt[:, e : e + 1] if e < NB else turned[:, 1 + 8 * (e - NB) : 2 + 8 * (e - NB)]
                high, low = split(jnp.where((lane % 32 == e) & (lane < 96), col, 0.0))
                xh[e, :, BLK:] = high
                xl[e, :, BLK:] = low

    for b in range(per):
        sh, sl, vh, vl = [], [], [], []
        for k in range(KB):
            col = cols_ref[step * per + b, k]
            high, low = split(s_ref[b, k])
            sh.append(high)
            sl.append(low)
            vh.append(xh[col])
            vl.append(xl[col])
        sh = jnp.concatenate(sh, axis=1)
        sl = jnp.concatenate(sl, axis=1)
        vh = jnp.concatenate(vh, axis=0)
        vl = jnp.concatenate(vl, axis=0)
        image = dot(sh, vh) + (dot(sh, vl) + dot(sl, vh))
        out_ref[b] = image[:, :BLK]
        if first:
            q = image[:, BLK:]
            high = q.astype(BF16)
            low = (q - high.astype(F32)).astype(BF16)
            lane = lax.broadcasted_iota(jnp.int32, (BLK, BLK), 1)
            q_ref[b] = jnp.where((lane >= 32) & (lane < 64), low.astype(F32), high.astype(F32)).astype(BF16)


def pack(u):
    keep = lax.broadcasted_iota(jnp.int32, (ROWS, BLK), 0) < EXT
    u = jnp.concatenate([jnp.where(keep, u, 0.0), jnp.zeros((32 - ROWS, BLK), F32)], axis=0)
    high, low = split(u)
    return jnp.concatenate([high, high, low, jnp.zeros((32, BLK), BF16)], axis=0)


def fold(x):
    return jnp.sum(x.reshape(BLK // 8, 8, BLK), axis=0)


def message(msg_ref, rows, dots):
    sums = [jnp.sum(d, axis=0, keepdims=True) for d in dots]
    zero = jnp.zeros((1, BLK), F32)
    tail = [zero] * (EXT - NB) + sums + [zero] * (ROWS - EXT - len(dots))
    block = jnp.concatenate(rows + tail, axis=0)
    for a in range(msg_ref.shape[0]):
        msg_ref[a] = block


def first_kernel(got_ref, r_ref, dr_ref, adr_ref, q_ref, w_ref, msg_ref, u_ref, z_ref, im_ref):
    u = jnp.sum(got_ref[...], axis=0)
    u_ref[...] = u
    packed = pack(u)
    wt = w_ref[...].T
    rows = []
    rz = jnp.zeros((8, BLK), F32)
    zw = jnp.zeros((8, BLK), F32)
    for i in range(NB):
        col = wt[:, i : i + 1]
        image = adr_ref[i] + dot(q_ref[i], packed)
        z = dr_ref[i] + col * u[i : i + 1]
        im_ref[i] = image
        z_ref[i] = z
        rows.append(jnp.sum(col * image, axis=0, keepdims=True))
        rz = rz + fold(r_ref[i] * z)
        zw = zw + fold(z * image)
    message(msg_ref, rows, [rz, zw])


def second_kernel(
    got_ref, u_ref, r_ref, z0_ref, im_ref, dr_ref, dim_ref, adr_ref, adim_ref, q_ref, w_ref,
    msg_ref, v_ref, r1_ref, dr1_ref, z1_ref, az_ref,
):
    v = jnp.sum(got_ref[...], axis=0)
    v_ref[...] = v
    alpha = v[EXT : EXT + 1] / v[EXT + 1 : EXT + 2]
    u = u_ref[...] - alpha * v
    packed = pack(u)
    wt = w_ref[...].T
    rows = []
    rz = jnp.zeros((8, BLK), F32)
    zaz = jnp.zeros((8, BLK), F32)
    cross = jnp.zeros((8, BLK), F32)
    for i in range(NB):
        col = wt[:, i : i + 1]
        image = im_ref[i]
        r1 = r_ref[i] - alpha * image
        dr1 = dr_ref[i] - alpha * dim_ref[i]
        z1 = dr1 + col * u[i : i + 1]
        az = adr_ref[i] - alpha * adim_ref[i] + dot(q_ref[i], packed)
        r1_ref[i] = r1
        dr1_ref[i] = dr1
        z1_ref[i] = z1
        az_ref[i] = az
        rows.append(jnp.sum(col * az, axis=0, keepdims=True))
        rz = rz + fold(r1 * z1)
        zaz = zaz + fold(z1 * az)
        cross = cross + fold(z1 * image + z0_ref[i] * az)
    message(msg_ref, rows, [rz, zaz, cross])


def image_kernel(f_ref, d_ref, out_ref):
    for i in range(NB):
        out_ref[i] = dot3(d_ref[i], f_ref[i])


def last_kernel(
    got_ref, u_ref, v_ref, r1_ref, dr1_ref, z0_ref, z1_ref, im_ref, dim_ref, az_ref, daz_ref, w_ref,
    sol_ref, res_ref, pre_ref,
):
    t = jnp.sum(got_ref[...], axis=0)
    v = v_ref[...]
    gamma0 = v[EXT : EXT + 1]
    curve0 = v[EXT + 1 : EXT + 2]
    gamma1 = t[EXT : EXT + 1]
    alpha0 = gamma0 / curve0
    beta = gamma1 / gamma0
    curve1 = t[EXT + 1 : EXT + 2] + beta * (t[EXT + 2 : EXT + 3] + beta * curve0)
    alpha1 = gamma1 / curve1
    u = u_ref[...] - alpha0 * v - alpha1 * (t + beta * v)
    wt = w_ref[...].T
    for i in range(NB):
        z0 = z0_ref[i]
        p1 = z1_ref[i] + beta * z0
        sol_ref[i] = alpha0 * z0 + alpha1 * p1
        res_ref[i] = r1_ref[i] - alpha1 * (az_ref[i] + beta * im_ref[i])
        local = dr1_ref[i] - alpha1 * (daz_ref[i] + beta * dim_ref[i])
        pre_ref[i] = local + wt[:, i : i + 1] * u[i : i + 1]


FIELD = (NB, BLK, BLK)


def vmem_specs(n):
    return [pl.BlockSpec(memory_space=pltpu.VMEM)] * n


def smem_spec():
    return pl.BlockSpec(memory_space=pltpu.SMEM)


def whole(shape):
    return pl.BlockSpec(shape, lambda i: (0,) * len(shape))


def apply_operator(stiffness, columns, field, lower, upper, weights=None):
    first = weights is not None
    per = 2
    wide = 2 * BLK if first else BLK
    block = pl.BlockSpec((per, BLK, BLK), lambda i: (i, 0, 0))
    outs = [jax.ShapeDtypeStruct(FIELD, F32)]
    args = [columns, stiffness, field, lower, upper]
    specs = [
        smem_spec(),
        pl.BlockSpec((per, KB, BLK, BLK), lambda i: (i, 0, 0, 0)),
        whole(FIELD),
        whole(lower.shape),
        whole(upper.shape),
    ]
    if first:
        outs.append(jax.ShapeDtypeStruct(FIELD, BF16))
        args.append(weights)
        specs.append(whole(weights.shape))
    return pl.pallas_call(
        functools.partial(operator_kernel, first),
        grid=(NB // per,),
        out_shape=outs,
        in_specs=specs,
        out_specs=[block] * len(outs),
        scratch_shapes=[pltpu.VMEM((EXT, BLK, wide), BF16)] * 2,
        compiler_params=pltpu.CompilerParams(vmem_limit_bytes=VMEM),
        cost_estimate=pl.CostEstimate(flops=6 * 10**9, bytes_accessed=8 << 20, transcendentals=0),
    )(*args)


def on_device(
    loads, stiffness, inv_diag, columns, send_lists, restrict_weights, coarse_map, coarse_diag
):
    devices = lax.axis_size(RING)
    gathered = lax.axis_size(GATHER)
    scattered = lax.axis_size(SCATTER)
    up = [(i, (i + 1) % devices) for i in range(devices)]
    down = [(j, i) for i, j in up]
    send = send_lists.reshape(1, 2)
    cells = coarse_map.astype(F32)
    msg_shape = ((gathered, ROWS, BLK), F32)
    part_shape = ((scattered, ROWS, BLK), F32)

    lane = jnp.arange(BLK, dtype=jnp.int32)
    mine = lane // NB == lax.axis_index(GATHER) % 8
    cell_rows = jnp.zeros((ROWS - NB, BLK), F32).at[0].set(jnp.where(mine, jnp.tile(cells, BLK // NB), 0.0))
    info = jnp.stack(
        [
            jnp.broadcast_to(cells[send[0], None], (2, BLK)),
            restrict_weights[send[0]],
        ],
        axis=1,
    )
    info = jnp.pad(info, ((0, 0), (0, 6), (0, 0)))

    (msg,) = call(restrict_kernel, [msg_shape], specs=vmem_specs(3), flops=10**6, moved=2 << 20)(
        loads, restrict_weights, cell_rows
    )
    packet = ((BLK + 8, BLK), F32)
    local, to_prev, to_next = call(
        local_kernel,
        [(FIELD, F32), packet, packet],
        specs=[smem_spec()] + vmem_specs(4),
        flops=2 * 10**8,
        moved=3 << 20,
    )(send, loads, inv_diag, restrict_weights, info)
    lower = lax.ppermute(to_next, RING, up)
    upper = lax.ppermute(to_prev, RING, down)

    target = jnp.concatenate(
        [
            jnp.broadcast_to(cells[:, None], (NB, BLK)),
            lower[BLK : BLK + 1],
            upper[BLK : BLK + 1],
            jnp.full((ROWS - EXT, BLK), -1.0, F32),
        ]
    )
    targets = lax.all_to_all(
        jnp.broadcast_to(target[None], part_shape[0]), SCATTER, 0, 0, tiled=True
    ).reshape(scattered * ROWS, BLK)
    (coarse_rows,) = call(
        sweep_kernel,
        [((CROWS, scattered * ROWS, BLK), F32)],
        specs=vmem_specs(2),
        flops=10**8,
        moved=2 << 20,
    )(targets, coarse_diag)
    got = lax.all_to_all(msg, GATHER, 0, 0, tiled=True)
    image_local, coupling = apply_operator(
        stiffness, columns, local, lower, upper, restrict_weights
    )
    weights_shape = ((scattered * ROWS, gathered * NB), BF16)
    cells_all = CROWS * BLK
    part, wh, wl = call(
        coarse_kernel,
        [part_shape, weights_shape, weights_shape],
        scratch=[
            pltpu.VMEM((scattered * ROWS, cells_all), BF16),
            pltpu.VMEM((scattered * ROWS, cells_all), BF16),
            pltpu.VMEM((cells_all, gathered * NB), BF16),
        ],
        specs=vmem_specs(2),
        flops=10**9,
        moved=2 << 20,
    )(coarse_rows, got)
    got = lax.all_to_all(part, SCATTER, 0, 0, tiled=True)

    msg, u0, z0, image0 = call(
        first_kernel,
        [msg_shape, (part_shape[0][1:], F32), (FIELD, F32), (FIELD, F32)],
        specs=vmem_specs(6),
        flops=10**8,
        moved=6 << 20,
    )(got, loads, local, image_local, coupling, restrict_weights)

    local_image, to_prev, to_next = call(
        local_kernel,
        [(FIELD, F32), packet, packet],
        specs=[smem_spec()] + vmem_specs(4),
        flops=2 * 10**8,
        moved=3 << 20,
    )(send, image0, inv_diag, restrict_weights, info)
    lower = lax.ppermute(to_next, RING, up)
    upper = lax.ppermute(to_prev, RING, down)
    (image_image,) = apply_operator(stiffness, columns, local_image, lower, upper)

    def exchange(msg):
        got = lax.all_to_all(msg, GATHER, 0, 0, tiled=True)
        (part,) = call(
            apply_kernel, [part_shape], specs=vmem_specs(3), flops=10**8, moved=1 << 20
        )(wh, wl, got)
        return lax.all_to_all(part, SCATTER, 0, 0, tiled=True)

    got = exchange(msg)
    msg, v0, residual1, local1, z1, image1 = call(
        second_kernel,
        [msg_shape, (part_shape[0][1:], F32)] + [(FIELD, F32)] * 4,
        specs=vmem_specs(11),
        flops=10**8,
        moved=12 << 20,
    )(
        got, u0, loads, z0, image0, local, local_image, image_local, image_image, coupling,
        restrict_weights,
    )
    (local_image1,) = call(
        image_kernel, [(FIELD, F32)], specs=vmem_specs(2), flops=2 * 10**8, moved=3 << 20
    )(image1, inv_diag)
    got = exchange(msg)
    return tuple(
        call(
            last_kernel, [(FIELD, F32)] * 3, specs=vmem_specs(12), flops=10**8, moved=12 << 20
        )(
            got, u0, v0, residual1, local1, z0, z1, image0, local_image, image1, local_image1,
            restrict_weights,
        )
    )


def solution(mesh):
    chips = mesh.devices.reshape(4, 8, 2, mesh.shape["crs"])
    fine = Mesh(chips, RING)
    placed = P(RING)
    return jax.shard_map(
        on_device,
        mesh=fine,
        in_specs=(placed,) * 7 + (P(),),
        out_specs=(placed,) * 3,
        check_vma=False,
    )
```

```python
import functools

import jax
import jax.numpy as jnp
from jax import lax
from jax.experimental import pallas as pl
from jax.experimental.pallas import tpu as pltpu
from jax.sharding import Mesh, PartitionSpec as P

OMEGA = 0.8
SWEEPS = 4
NB = 16
BLK = 128
KB = 6
EXT = 18
ROWS = 24
CROWS = 16
RING = ("y", "z", "core", "crs")
GATHER = ("y", "z")
SCATTER = ("core", "crs")
F32 = jnp.float32
BF16 = jnp.bfloat16
BIG = 60 * 1024 * 1024
SMALL = 12 * 1024 * 1024
TROWS = 32
CHUNK = 4


def sweep_coefficients():
    total = [0.0] * SWEEPS
    power = [1.0]
    for _ in range(SWEEPS):
        for i, c in enumerate(power):
            total[i] += c
        grown = [0.0] * (len(power) + 1)
        for i, c in enumerate(power):
            grown[i] += c * (1.0 - OMEGA)
            grown[i + 1] += c * OMEGA
        power = grown
    return total


def split(x):
    high = x.astype(BF16)
    return high, (x - high.astype(F32)).astype(BF16)


def dot(a, b):
    return jnp.dot(a, b, preferred_element_type=F32)


def dot3(a, b):
    ah, al = split(a)
    bh, bl = split(b)
    return dot(ah, bh) + (dot(ah, bl) + dot(al, bh))


def staged(body, ins, outs, scratch=(), flops=0, moved=0, limit=BIG):
    kinds_in = [k for _, k in ins]
    kinds_out = [k for _, _, k in outs]
    n_in, n_out = len(ins), len(outs)
    parts = NB // CHUNK

    def buffer(shape, dtype, kind):
        return pltpu.SMEM(shape, dtype) if kind == "scalar" else pltpu.VMEM(shape, dtype)

    buffers = [buffer(a.shape, a.dtype, k) for a, k in ins if k not in ("vmem", "hbm")]
    buffers += [buffer(sh, dt, k) for sh, dt, k in outs if k != "vmem"]

    def kernel(*refs):
        sources, targets = refs[:n_in], refs[n_in : n_in + n_out]
        rest = list(refs[n_in + n_out :])
        sem_in, sem_out = rest.pop(), rest.pop()
        bufs_in = [r if k in ("vmem", "hbm") else rest.pop(0) for r, k in zip(sources, kinds_in)]
        bufs_out = [r if k == "vmem" else rest.pop(0) for r, k in zip(targets, kinds_out)]

        def chunk(ref, c):
            return ref.at[pl.ds(c * CHUNK, CHUNK)]

        first = [
            pltpu.make_async_copy(s, b, sem_in.at[j, 0])
            for j, (s, b, k) in enumerate(zip(sources, bufs_in, kinds_in))
            if k in ("whole", "scalar")
        ]
        fields = [
            [
                pltpu.make_async_copy(chunk(s, c), chunk(b, c), sem_in.at[j, c])
                for j, (s, b, k) in enumerate(zip(sources, bufs_in, kinds_in))
                if k == "field"
            ]
            for c in range(parts)
        ]
        for copy in first + sum(fields, []):
            copy.start()
        sent = []

        def ready(c):
            for copy in fields[c]:
                copy.wait()

        def emit(n, c=0):
            if kinds_out[n] == "field":
                copy = pltpu.make_async_copy(chunk(bufs_out[n], c), chunk(targets[n], c), sem_out.at[n, c])
            else:
                copy = pltpu.make_async_copy(bufs_out[n], targets[n], sem_out.at[n, 0])
            copy.start()
            sent.append(copy)

        for copy in first:
            copy.wait()
        body(ready, emit, *bufs_in, *bufs_out, *rest)
        for copy in sent:
            copy.wait()

    def spec(kind):
        return pl.BlockSpec(memory_space=pltpu.VMEM if kind == "vmem" else pltpu.HBM)

    return pl.pallas_call(
        kernel,
        out_shape=[jax.ShapeDtypeStruct(sh, dt) for sh, dt, _ in outs],
        in_specs=[spec(k) for k in kinds_in],
        out_specs=[spec(k) for k in kinds_out],
        scratch_shapes=buffers
        + list(scratch)
        + [pltpu.SemaphoreType.DMA((n_out, parts)), pltpu.SemaphoreType.DMA((n_in, parts))],
        compiler_params=pltpu.CompilerParams(vmem_limit_bytes=limit),
        cost_estimate=pl.CostEstimate(flops=flops, bytes_accessed=moved, transcendentals=0),
    )(*[a for a, _ in ins])


def column_cells(map_ref):
    rows = [jnp.full((1, BLK), map_ref[i], jnp.int32) for i in range(NB)]
    return jnp.concatenate(rows, axis=0).astype(F32)


def broadcast(msg_ref, rows):
    for a in range(msg_ref.shape[0]):
        msg_ref[a] = rows


def chunks():
    return [(c, range(c * CHUNK, (c + 1) * CHUNK)) for c in range(NB // CHUNK)]


def start_body(ready, emit, map_ref, w_ref, r_ref, rows_ref):
    wt = w_ref[...].T
    lane = lax.broadcasted_iota(jnp.int32, (1, BLK), 1)
    cells = jnp.zeros((1, BLK), jnp.int32)
    for i in range(NB):
        cells = jnp.where(lane % NB == i, map_ref[i], cells)
    mine = lane // NB == lax.axis_index(GATHER) % 8
    cells = jnp.where(mine, cells, 0).astype(F32)
    rows = []
    for c, blocks in chunks():
        ready(c)
        rows += [jnp.sum(wt[:, i : i + 1] * r_ref[i], axis=0, keepdims=True) for i in blocks]
    rows_ref[...] = jnp.concatenate(rows + [cells, jnp.zeros((ROWS - NB - 1, BLK), F32)], axis=0)


def group_ghosts(t_ref):
    return jnp.sum(t_ref[:, NB:, :], axis=0)


def open_body(ready, emit, rows_ref, t_ref, msg_ref):
    ghosts = group_ghosts(t_ref)
    rows = jnp.concatenate(
        [rows_ref[: NB + 1], ghosts[:1], ghosts[NB - 1 :], rows_ref[NB + 3 :]], axis=0
    )
    broadcast(msg_ref, rows)
    emit(0)


def local_body(ready, emit, send_ref, w_ref, r_ref, d_ref, out_ref, prev_ref, next_ref):
    for c, blocks in chunks():
        ready(c)
        for i in blocks:
            out_ref[i] = dot3(d_ref[i], r_ref[i])
        emit(0, c)
    for slot, ref in ((0, prev_ref), (1, next_ref)):
        block = send_ref[0, slot]
        ref[:BLK] = out_ref[block]
        ref[BLK:] = jnp.concatenate(
            [w_ref[pl.ds(block, 1), :], jnp.zeros((7, BLK), F32)], axis=0
        )


def target_body(ready, emit, send_ref, map_ref, out_ref):
    slots = 2 * out_ref.shape[0]
    place = lax.axis_index(SCATTER)
    row = lax.broadcasted_iota(jnp.int32, (slots, BLK), 0)
    to_next = jnp.full((slots, BLK), map_ref[send_ref[0, 1]], jnp.int32)
    to_prev = jnp.full((slots, BLK), map_ref[send_ref[0, 0]], jnp.int32)
    ghosts = jnp.where(row == (2 * place + 2) % slots, to_next, 0)
    ghosts = jnp.where(row == (2 * place + slots - 1) % slots, to_prev, ghosts).astype(F32)
    own = column_cells(map_ref)
    for a in range(out_ref.shape[0]):
        out_ref[a, :NB] = own
        out_ref[a, NB:] = ghosts
    emit(0)


def image_body(ready, emit, send_ref, f_ref, d_ref, out_ref, prev_ref, next_ref):
    for c, blocks in chunks():
        ready(c)
        for i in blocks:
            out_ref[i] = dot3(d_ref[i], f_ref[i])
        emit(0, c)
    for slot, ref in ((0, prev_ref), (1, next_ref)):
        ref[...] = out_ref[send_ref[0, slot]]


def product_body(ready, emit, f_ref, d_ref, out_ref):
    for c, blocks in chunks():
        ready(c)
        for i in blocks:
            out_ref[i] = dot3(d_ref[i], f_ref[i])
        emit(0, c)


def solve_rows(cell, inv, use):
    coef = sweep_coefficients()
    lane = lax.broadcasted_iota(jnp.int32, (8, BLK), 1)
    spot = [jnp.where(cell == (lane + BLK * r).astype(F32), 1.0, 0.0) for r in range(CROWS)]
    t = [coef[-1] * spot[r] for r in range(CROWS)]
    for power in range(SWEEPS - 2, -1, -1):
        y = [t[r] * inv[r : r + 1] for r in range(CROWS)]
        new = []
        for r in range(CROWS):
            v = jnp.where(lane == 0, 0.0, pltpu.roll(y[r], 1, 1))
            v = v + jnp.where(lane == BLK - 1, 0.0, pltpu.roll(y[r], BLK - 1, 1))
            if r > 0:
                v = v + y[r - 1]
            if r < CROWS - 1:
                v = v + y[r + 1]
            new.append(v + coef[power] * spot[r])
        t = new
    for r in range(CROWS):
        use(r, t[r] * (inv[r : r + 1] * OMEGA))


def sweep_body(ready, emit, t_ref, diag_ref, out_ref, cell_ref):
    inv = 1.0 / (4.0 + diag_ref[...])
    devs = t_ref.shape[0]
    for g in range(devs):
        cell_ref[g * NB : (g + 1) * NB] = t_ref[g, :NB]
    slots = 2 * devs
    row = lax.broadcasted_iota(jnp.int32, (slots, BLK), 0)
    inner = (row > 0) & (row < slots - 1)
    cell_ref[devs * NB :] = jnp.where(inner, group_ghosts(t_ref), -1.0)

    def chunk(c, _):
        here = pl.ds(pl.multiple_of(c * 8, 8), 8)

        def use(r, value):
            out_ref[r, here, :] = value

        solve_rows(cell_ref[here, :], inv, use)
        return 0

    lax.fori_loop(0, cell_ref.shape[0] // 8, chunk, 0)
    emit(0)


def spread(part, sums, part_ref):
    devs = part_ref.shape[0]
    part_ref[:, :NB, :] = part[: devs * NB].reshape(devs, NB, BLK)
    for g in range(devs):
        ghosts = part[devs * NB + 2 * g : devs * NB + 2 * g + 2]
        part_ref[g, NB:, :] = jnp.concatenate([ghosts, sums[EXT - NB :]], axis=0)


def coarse_body(
    ready, emit, rows_hbm, diag_ref, g_ref, part_ref, wh_ref, wl_ref, rows_ref, sh_ref, sl_ref, oh_ref, sem
):
    copy = pltpu.make_async_copy(rows_hbm, rows_ref, sem)
    copy.start()
    devs = g_ref.shape[0]
    sources = devs * NB
    cells = g_ref[:, NB : NB + 1, :].reshape(devs, BLK)
    cells = jnp.sum(cells.reshape(devs // 8, 8, BLK), axis=1)
    sub = lax.broadcasted_iota(jnp.int32, (BLK, BLK), 0)
    for r in range(CROWS):
        index = (sub + r * BLK).astype(F32)
        for q in range(devs // 8):
            hit = jnp.where(cells[q : q + 1] == index, 1.0, 0.0)
            oh_ref[r * BLK : (r + 1) * BLK, q * BLK : (q + 1) * BLK] = hit.astype(BF16)
    place = lax.axis_index(GATHER)
    before = g_ref[(place + devs - 1) % devs][NB + 1 : NB + 2]
    after = g_ref[(place + 1) % devs][NB + 2 : NB + 3]
    row = lax.broadcasted_iota(jnp.int32, (8, BLK), 0)
    outer = jnp.where(row == 0, before, jnp.where(row == 7, after, -1.0))
    copy.wait()
    size = rows_ref.shape[1]
    base = size - NB

    def use(r, value):
        rows_ref[r, base : base + 8, :] += jnp.where(row == 0, value, 0.0)
        rows_ref[r, size - 8 :, :] += jnp.where(row == 7, value, 0.0)

    solve_rows(outer, 1.0 / (4.0 + diag_ref[...]), use)
    for r in range(CROWS):
        here = slice(r * BLK, (r + 1) * BLK)
        high, low = split(rows_ref[r])
        sh_ref[:, here] = high
        sl_ref[:, here] = low
    w = dot(sh_ref[...], oh_ref[...]) + dot(sl_ref[...], oh_ref[...])
    wh, wl = split(w)
    wh_ref[...] = wh
    wl_ref[...] = wl
    emit(1)
    emit(2)
    gh, gl = split(g_ref[:, :NB, :].reshape(sources, BLK))
    part = dot(wh, gh) + (dot(wh, gl) + dot(wl, gh))
    spread(part, jnp.zeros((ROWS - NB, BLK), F32), part_ref)
    emit(0)


def apply_body(ready, emit, wh_ref, wl_ref, g_ref, part_ref):
    devs = g_ref.shape[0]
    gh, gl = split(g_ref[:, :NB, :].reshape(devs * NB, BLK))
    wh = wh_ref[...]
    part = dot(wh, gh) + (dot(wh, gl) + dot(wl_ref[...], gh))
    spread(part, jnp.sum(g_ref[:, NB:, :], axis=0), part_ref)
    emit(0)


def operator_kernel(first, cols_ref, s_ref, f_ref, lo_ref, up_ref, *rest):
    if first:
        w_ref, out_ref, q_ref, xh, xl = rest
    else:
        out_ref, xh, xl = rest
    step = pl.program_id(0)
    per = s_ref.shape[0]

    @pl.when(step == 0)
    def _():
        if first:
            wt = w_ref[...].T
            lane = lax.broadcasted_iota(jnp.int32, (BLK, BLK), 1)
            turned = jnp.concatenate(
                [lo_ref[BLK:, :], up_ref[BLK:, :]], axis=0
            ).T
        for e in range(EXT):
            x = f_ref[e] if e < NB else (lo_ref, up_ref)[e - NB][:BLK, :]
            high, low = split(x)
            xh[e, :, :BLK] = high
            xl[e, :, :BLK] = low
            if first:
                col = wt[:, e : e + 1] if e < NB else turned[:, 8 * (e - NB) : 1 + 8 * (e - NB)]
                high, low = split(jnp.where((lane % 32 == e) & (lane < 96), col, 0.0))
                xh[e, :, BLK:] = high
                xl[e, :, BLK:] = low

    for b in range(per):
        sh, sl, vh, vl = [], [], [], []
        for k in range(KB):
            col = cols_ref[k, step * per + b]
            high, low = split(s_ref[b, k])
            sh.append(high)
            sl.append(low)
            vh.append(xh[col])
            vl.append(xl[col])
        sh = jnp.concatenate(sh, axis=1)
        sl = jnp.concatenate(sl, axis=1)
        vh = jnp.concatenate(vh, axis=0)
        vl = jnp.concatenate(vl, axis=0)
        image = dot(sh, vh) + (dot(sh, vl) + dot(sl, vh))
        out_ref[b] = image[:, :BLK]
        if first:
            q = image[:, BLK:]
            high = q.astype(BF16)
            low = (q - high.astype(F32)).astype(BF16)
            lane = lax.broadcasted_iota(jnp.int32, (BLK, BLK), 1)
            q_ref[b] = jnp.where((lane >= 32) & (lane < 64), low.astype(F32), high.astype(F32)).astype(BF16)


def pack(u):
    keep = lax.broadcasted_iota(jnp.int32, (ROWS, BLK), 0) < EXT
    u = jnp.concatenate([jnp.where(keep, u, 0.0), jnp.zeros((32 - ROWS, BLK), F32)], axis=0)
    high, low = split(u)
    return jnp.concatenate([high, high, low, jnp.zeros((32, BLK), BF16)], axis=0)


def fold(x):
    return jnp.sum(x.reshape(BLK // 8, 8, BLK), axis=0)


def message(rows, dots):
    sums = [jnp.sum(d, axis=0, keepdims=True) for d in dots]
    zero = jnp.zeros((1, BLK), F32)
    end = [zero] * (EXT - NB) + sums + [zero] * (ROWS - EXT - len(dots))
    return jnp.concatenate(rows + end, axis=0)


def first_body(ready, emit, got_ref, w_ref, r_ref, dr_ref, adr_ref, q_ref, msg_ref, u_ref, im_ref):
    u = jnp.sum(got_ref[...], axis=0)
    u_ref[...] = u
    emit(1)
    packed = pack(u)
    wt = w_ref[...].T
    rows = []
    rz = jnp.zeros((8, BLK), F32)
    zw = jnp.zeros((8, BLK), F32)
    for c, blocks in chunks():
        ready(c)
        for i in blocks:
            col = wt[:, i : i + 1]
            image = adr_ref[i] + dot(q_ref[i], packed)
            z = dr_ref[i] + col * u[i : i + 1]
            im_ref[i] = image
            rows.append(jnp.sum(col * image, axis=0, keepdims=True))
            rz = rz + fold(r_ref[i] * z)
            zw = zw + fold(z * image)
        emit(2, c)
    broadcast(msg_ref, message(rows, [rz, zw]))
    emit(0)


def second_body(
    ready, emit, got_ref, u_ref, w_ref, r_ref, im_ref, dr_ref, dim_ref, adr_ref, adim_ref, q_ref,
    msg_ref, v_ref, az_ref,
):
    v = jnp.sum(got_ref[...], axis=0)
    v_ref[...] = v
    emit(1)
    alpha = v[EXT : EXT + 1] / v[EXT + 1 : EXT + 2]
    u0 = u_ref[...]
    u = u0 - alpha * v
    packed = pack(u)
    wt = w_ref[...].T
    rows = []
    rz = jnp.zeros((8, BLK), F32)
    zaz = jnp.zeros((8, BLK), F32)
    cross = jnp.zeros((8, BLK), F32)
    for c, blocks in chunks():
        ready(c)
        for i in blocks:
            col = wt[:, i : i + 1]
            image = im_ref[i]
            dr = dr_ref[i]
            z0 = dr + col * u0[i : i + 1]
            z1 = dr - alpha * dim_ref[i] + col * u[i : i + 1]
            az = adr_ref[i] - alpha * adim_ref[i] + dot(q_ref[i], packed)
            az_ref[i] = az
            rows.append(jnp.sum(col * az, axis=0, keepdims=True))
            rz = rz + fold((r_ref[i] - alpha * image) * z1)
            zaz = zaz + fold(z1 * az)
            cross = cross + fold(z1 * image + z0 * az)
        emit(2, c)
    broadcast(msg_ref, message(rows, [rz, zaz, cross]))
    emit(0)


def last_body(
    ready, emit, got_ref, u_ref, v_ref, w_ref, r_ref, im_ref, dr_ref, dim_ref, az_ref, daz_ref,
    sol_ref, res_ref, pre_ref,
):
    t = jnp.sum(got_ref[...], axis=0)
    v = v_ref[...]
    gamma0 = v[EXT : EXT + 1]
    curve0 = v[EXT + 1 : EXT + 2]
    gamma1 = t[EXT : EXT + 1]
    alpha0 = gamma0 / curve0
    beta = gamma1 / gamma0
    curve1 = t[EXT + 1 : EXT + 2] + beta * (t[EXT + 2 : EXT + 3] + beta * curve0)
    alpha1 = gamma1 / curve1
    u0 = u_ref[...]
    u1 = u0 - alpha0 * v
    u2 = u1 - alpha1 * (t + beta * v)
    wt = w_ref[...].T
    for c, blocks in chunks():
        ready(c)
        for i in blocks:
            col = wt[:, i : i + 1]
            image = im_ref[i]
            dr = dr_ref[i]
            dim = dim_ref[i]
            z0 = dr + col * u0[i : i + 1]
            dr1 = dr - alpha0 * dim
            z1 = dr1 + col * u1[i : i + 1]
            sol_ref[i] = alpha0 * z0 + alpha1 * (z1 + beta * z0)
            res_ref[i] = r_ref[i] - alpha0 * image - alpha1 * (az_ref[i] + beta * image)
            local = dr1 - alpha1 * (daz_ref[i] + beta * dim)
            pre_ref[i] = local + col * u2[i : i + 1]
        for n in range(3):
            emit(n, c)


FIELD = (NB, BLK, BLK)


def block_of(shape):
    return pl.BlockSpec(shape, lambda i: (0,) * len(shape))


def apply_operator(stiffness, columns, field, lower, upper, weights=None):
    first = weights is not None
    per = 4
    wide = 2 * BLK if first else BLK
    block = pl.BlockSpec((per, BLK, BLK), lambda i: (i, 0, 0))
    outs = [jax.ShapeDtypeStruct(FIELD, F32)]
    args = [columns, stiffness, field, lower, upper]
    specs = [
        pl.BlockSpec(memory_space=pltpu.SMEM),
        pl.BlockSpec((per, KB, BLK, BLK), lambda i: (i, 0, 0, 0)),
        block_of(FIELD),
        block_of(lower.shape),
        block_of(upper.shape),
    ]
    if first:
        outs.append(jax.ShapeDtypeStruct(FIELD, BF16))
        args.append(weights)
        specs.append(block_of(weights.shape))
    return pl.pallas_call(
        functools.partial(operator_kernel, first),
        grid=(NB // per,),
        out_shape=outs,
        in_specs=specs,
        out_specs=[block] * len(outs),
        scratch_shapes=[pltpu.VMEM((EXT, BLK, wide), BF16)] * 2,
        compiler_params=pltpu.CompilerParams(vmem_limit_bytes=BIG),
        cost_estimate=pl.CostEstimate(flops=6 * 10**9, bytes_accessed=8 << 20, transcendentals=0),
    )(*args)


def on_device(
    loads, stiffness, inv_diag, columns, send_lists, restrict_weights, coarse_map, coarse_diag
):
    devices = lax.axis_size(RING)
    gathered = lax.axis_size(GATHER)
    scattered = lax.axis_size(SCATTER)
    up = [(i, (i + 1) % devices) for i in range(devices)]
    down = [(j, i) for i, j in up]
    send = (send_lists.reshape(1, 2), "scalar")
    cells = (coarse_map, "scalar")
    columns = columns.T
    weights = (restrict_weights, "whole")
    msg_out = ((gathered, ROWS, BLK), F32, "whole")
    part_shape = (scattered, ROWS, BLK)
    part_out = (part_shape, F32, "whole")
    short_out = (part_shape[1:], F32, "whole")
    field_out = (FIELD, F32, "field")
    big = 2 << 20

    (target,) = staged(
        target_body,
        [send, cells],
        [((scattered, TROWS, BLK), F32, "whole")],
        moved=1 << 18,
        limit=SMALL,
    )
    targets = lax.all_to_all(target, SCATTER, 0, 0, tiled=True)
    (start_rows,) = staged(
        start_body,
        [cells, weights, (loads, "field")],
        [((ROWS, BLK), F32, "vmem")],
        flops=10**6,
        moved=big,
    )
    (msg,) = staged(
        open_body, [(start_rows, "vmem"), (targets, "vmem")], [msg_out], moved=1 << 18, limit=SMALL
    )
    got = lax.all_to_all(msg, GATHER, 0, 0, tiled=True)
    packet = ((BLK + 8, BLK), F32, "vmem")
    local, to_prev, to_next = staged(
        local_body,
        [send, weights, (loads, "field"), (inv_diag, "field")],
        [field_out, packet, packet],
        flops=2 * 10**8,
        moved=big,
    )
    lower = lax.ppermute(to_next, RING, up)
    upper = lax.ppermute(to_prev, RING, down)
    rows = scattered * EXT
    (coarse_rows,) = staged(
        sweep_body,
        [(targets, "vmem"), (coarse_diag, "whole")],
        [((CROWS, rows, BLK), F32, "whole")],
        scratch=[pltpu.VMEM((rows, BLK), F32)],
        flops=10**8,
        moved=big,
        limit=SMALL,
    )
    image_local, coupling = apply_operator(
        stiffness, columns, local, lower, upper, restrict_weights
    )
    weights_out = ((rows, gathered * NB), BF16, "whole")
    cells_all = CROWS * BLK
    part, wh, wl = staged(
        coarse_body,
        [(coarse_rows, "hbm"), (coarse_diag, "whole"), (got, "vmem")],
        [part_out, weights_out, weights_out],
        scratch=[
            pltpu.VMEM((CROWS, rows, BLK), F32),
            pltpu.VMEM((rows, cells_all), BF16),
            pltpu.VMEM((rows, cells_all), BF16),
            pltpu.VMEM((cells_all, gathered * NB), BF16),
            pltpu.SemaphoreType.DMA(()),
        ],
        flops=10**9,
        moved=big,
        limit=SMALL,
    )
    got = lax.all_to_all(part, SCATTER, 0, 0, tiled=True)

    msg, u0, image0 = staged(
        first_body,
        [(got, "vmem"), weights, (loads, "field"), (local, "field"), (image_local, "field"),
         (coupling, "field")],
        [msg_out, short_out, field_out],
        flops=10**8,
        moved=big,
    )
    packet = ((BLK, BLK), F32, "vmem")
    local_image, to_prev, to_next = staged(
        image_body,
        [send, (image0, "field"), (inv_diag, "field")],
        [field_out, packet, packet],
        flops=2 * 10**8,
        moved=big,
    )
    lower = lax.ppermute(to_next, RING, up)
    upper = lax.ppermute(to_prev, RING, down)
    (image_image,) = apply_operator(stiffness, columns, local_image, lower, upper)

    def exchange(msg):
        got = lax.all_to_all(msg, GATHER, 0, 0, tiled=True)
        (part,) = staged(
            apply_body,
            [(wh, "whole"), (wl, "whole"), (got, "vmem")],
            [part_out],
            flops=10**8,
            moved=big,
            limit=SMALL,
        )
        return lax.all_to_all(part, SCATTER, 0, 0, tiled=True)

    got = exchange(msg)
    msg, v0, image1 = staged(
        second_body,
        [(got, "vmem"), (u0, "whole"), weights, (loads, "field"), (image0, "field"),
         (local, "field"), (local_image, "field"), (image_local, "field"),
         (image_image, "field"), (coupling, "field")],
        [msg_out, short_out, field_out],
        flops=10**8,
        moved=big,
    )
    (local_image1,) = staged(
        product_body,
        [(image1, "field"), (inv_diag, "field")],
        [field_out],
        flops=2 * 10**8,
        moved=big,
    )
    got = exchange(msg)
    return tuple(
        staged(
            last_body,
            [(got, "vmem"), (u0, "whole"), (v0, "whole"), weights, (loads, "field"),
             (image0, "field"), (local, "field"), (local_image, "field"), (image1, "field"),
             (local_image1, "field")],
            [field_out] * 3,
            flops=10**8,
            moved=big,
        )
    )


def solution(mesh):
    chips = mesh.devices.reshape(4, 8, 2, mesh.shape["crs"])
    fine = Mesh(chips, RING)
    placed = P(RING)
    return jax.shard_map(
        on_device,
        mesh=fine,
        in_specs=(placed,) * 7 + (P(),),
        out_specs=(placed,) * 3,
        check_vma=False,
    )
```

```python
import functools

import jax
import jax.numpy as jnp
from jax import lax
from jax.experimental import pallas as pl
from jax.experimental.pallas import tpu as pltpu
from jax.sharding import Mesh, PartitionSpec as P

OMEGA = 0.8
SWEEPS = 4
NB = 16
BLK = 128
KB = 6
EXT = 18
MROWS = 19
ROWS = 24
CROWS = 16
RING = ("y", "z", "core", "crs")
GATHER = ("y", "z")
SCATTER = ("core", "crs")
F32 = jnp.float32
BF16 = jnp.bfloat16
BIG = 60 * 1024 * 1024
SMALL = 12 * 1024 * 1024
TROWS = 32
GROUP = 4
CHUNK = 8


def sweep_coefficients():
    total = [0.0] * SWEEPS
    power = [1.0]
    for _ in range(SWEEPS):
        for i, c in enumerate(power):
            total[i] += c
        grown = [0.0] * (len(power) + 1)
        for i, c in enumerate(power):
            grown[i] += c * (1.0 - OMEGA)
            grown[i + 1] += c * OMEGA
        power = grown
    return total


def split(x):
    high = x.astype(BF16)
    return high, (x - high.astype(F32)).astype(BF16)


def dot(a, b):
    return jnp.dot(a, b, preferred_element_type=F32)


def dot3(a, b):
    ah, al = split(a)
    bh, bl = split(b)
    return dot(ah, bh) + (dot(ah, bl) + dot(al, bh))


def staged(body, ins, outs, scratch=(), flops=0, moved=0, limit=BIG):
    kinds_in = [k for _, k in ins]
    kinds_out = [k for _, _, k in outs]
    n_in, n_out = len(ins), len(outs)
    parts = NB // CHUNK

    def buffer(shape, dtype, kind):
        return pltpu.SMEM(shape, dtype) if kind == "scalar" else pltpu.VMEM(shape, dtype)

    buffers = [buffer(a.shape, a.dtype, k) for a, k in ins if k not in ("vmem", "hbm")]
    buffers += [buffer(sh, dt, k) for sh, dt, k in outs if k != "vmem"]

    def kernel(*refs):
        sources, targets = refs[:n_in], refs[n_in : n_in + n_out]
        rest = list(refs[n_in + n_out :])
        sem_in, sem_out = rest.pop(), rest.pop()
        bufs_in = [r if k in ("vmem", "hbm") else rest.pop(0) for r, k in zip(sources, kinds_in)]
        bufs_out = [r if k == "vmem" else rest.pop(0) for r, k in zip(targets, kinds_out)]

        def chunk(ref, c):
            return ref.at[pl.ds(c * CHUNK, CHUNK)]

        first = [
            pltpu.make_async_copy(s, b, sem_in.at[j, 0])
            for j, (s, b, k) in enumerate(zip(sources, bufs_in, kinds_in))
            if k in ("whole", "scalar")
        ]
        fields = [
            [
                pltpu.make_async_copy(chunk(s, c), chunk(b, c), sem_in.at[j, c])
                for j, (s, b, k) in enumerate(zip(sources, bufs_in, kinds_in))
                if k == "field"
            ]
            for c in range(parts)
        ]
        for copy in first + sum(fields, []):
            copy.start()
        sent = []

        def ready(c):
            for copy in fields[c]:
                copy.wait()

        def emit(n, c=0):
            if kinds_out[n] == "field":
                copy = pltpu.make_async_copy(chunk(bufs_out[n], c), chunk(targets[n], c), sem_out.at[n, c])
            else:
                copy = pltpu.make_async_copy(bufs_out[n], targets[n], sem_out.at[n, 0])
            copy.start()
            sent.append(copy)

        for copy in first:
            copy.wait()
        body(ready, emit, *bufs_in, *bufs_out, *rest)
        for copy in sent:
            copy.wait()

    def spec(kind):
        return pl.BlockSpec(memory_space=pltpu.VMEM if kind == "vmem" else pltpu.HBM)

    return pl.pallas_call(
        kernel,
        out_shape=[jax.ShapeDtypeStruct(sh, dt) for sh, dt, _ in outs],
        in_specs=[spec(k) for k in kinds_in],
        out_specs=[spec(k) for k in kinds_out],
        scratch_shapes=buffers
        + list(scratch)
        + [pltpu.SemaphoreType.DMA((n_out, parts)), pltpu.SemaphoreType.DMA((n_in, parts))],
        compiler_params=pltpu.CompilerParams(vmem_limit_bytes=limit),
        cost_estimate=pl.CostEstimate(flops=flops, bytes_accessed=moved, transcendentals=0),
    )(*[a for a, _ in ins])


def column_cells(map_ref):
    rows = [jnp.full((1, BLK), map_ref[i], jnp.int32) for i in range(NB)]
    return jnp.concatenate(rows, axis=0).astype(F32)


def broadcast(msg_ref, rows):
    for a in range(msg_ref.shape[0]):
        msg_ref[a] = rows


def chunks():
    return [(c, range(c * CHUNK, (c + 1) * CHUNK)) for c in range(NB // CHUNK)]


def start_body(ready, emit, map_ref, w_ref, r_ref, rows_ref):
    wt = w_ref[...].T
    lane = lax.broadcasted_iota(jnp.int32, (1, BLK), 1)
    cells = jnp.zeros((1, BLK), jnp.int32)
    for i in range(NB):
        cells = jnp.where(lane % NB == i, map_ref[i], cells)
    mine = lane // NB == lax.axis_index(GATHER) % 8
    cells = jnp.where(mine, cells, 0).astype(F32)
    rows = []
    for c, blocks in chunks():
        ready(c)
        rows += [jnp.sum(wt[:, i : i + 1] * r_ref[i], axis=0, keepdims=True) for i in blocks]
    rows_ref[...] = jnp.concatenate(rows + [cells, jnp.zeros((ROWS - NB - 1, BLK), F32)], axis=0)


def group_ghosts(t_ref):
    return jnp.sum(t_ref[:, NB:, :], axis=0)


def open_body(ready, emit, rows_ref, t_ref, msg_ref):
    ghosts = group_ghosts(t_ref)
    rows = jnp.concatenate([rows_ref[: NB + 1], ghosts[:1], ghosts[NB - 1 :]], axis=0)
    broadcast(msg_ref, rows)
    emit(0)


def slot_of(swap):
    return (lax.axis_index("crs") + 1 + swap) % 2


def local_body(ready, emit, send_ref, w_ref, r_ref, d_ref, out_ref, inner_ref, outer_ref):
    for c, blocks in chunks():
        ready(c)
        for i in blocks:
            out_ref[i] = dot3(d_ref[i], r_ref[i])
        emit(0, c)
    for n, ref in ((0, inner_ref), (1, outer_ref)):
        block = send_ref[0, slot_of(n)]
        ref[:BLK] = out_ref[block]
        ref[BLK:] = jnp.concatenate(
            [w_ref[pl.ds(block, 1), :], jnp.zeros((7, BLK), F32)], axis=0
        )


def target_body(ready, emit, send_ref, map_ref, out_ref):
    slots = 2 * out_ref.shape[0]
    place = lax.axis_index(SCATTER)
    row = lax.broadcasted_iota(jnp.int32, (slots, BLK), 0)
    to_next = jnp.full((slots, BLK), map_ref[send_ref[0, 1]], jnp.int32)
    to_prev = jnp.full((slots, BLK), map_ref[send_ref[0, 0]], jnp.int32)
    ghosts = jnp.where(row == (2 * place + 2) % slots, to_next, 0)
    ghosts = jnp.where(row == (2 * place + slots - 1) % slots, to_prev, ghosts).astype(F32)
    own = column_cells(map_ref)
    for a in range(out_ref.shape[0]):
        out_ref[a, :NB] = own
        out_ref[a, NB:] = ghosts
    emit(0)


def image_body(ready, emit, send_ref, f_ref, d_ref, out_ref, inner_ref, outer_ref):
    for c, blocks in chunks():
        ready(c)
        for i in blocks:
            out_ref[i] = dot3(d_ref[i], f_ref[i])
        emit(0, c)
    for n, ref in ((0, inner_ref), (1, outer_ref)):
        ref[...] = out_ref[send_ref[0, slot_of(n)]]


def product_body(ready, emit, f_ref, d_ref, out_ref):
    for c, blocks in chunks():
        ready(c)
        for i in blocks:
            out_ref[i] = dot3(d_ref[i], f_ref[i])
        emit(0, c)


def solve_rows(cell, inv, use):
    coef = sweep_coefficients()
    lane = lax.broadcasted_iota(jnp.int32, (8, BLK), 1)
    spot = [jnp.where(cell == (lane + BLK * r).astype(F32), 1.0, 0.0) for r in range(CROWS)]
    t = [coef[-1] * spot[r] for r in range(CROWS)]
    for power in range(SWEEPS - 2, -1, -1):
        y = [t[r] * inv[r : r + 1] for r in range(CROWS)]
        new = []
        for r in range(CROWS):
            v = jnp.where(lane == 0, 0.0, pltpu.roll(y[r], 1, 1))
            v = v + jnp.where(lane == BLK - 1, 0.0, pltpu.roll(y[r], BLK - 1, 1))
            if r > 0:
                v = v + y[r - 1]
            if r < CROWS - 1:
                v = v + y[r + 1]
            new.append(v + coef[power] * spot[r])
        t = new
    for r in range(CROWS):
        use(r, t[r] * (inv[r : r + 1] * OMEGA))


def sweep_body(ready, emit, t_ref, diag_ref, out_ref, cell_ref):
    inv = 1.0 / (4.0 + diag_ref[...])
    devs = t_ref.shape[0]
    for g in range(devs):
        cell_ref[g * NB : (g + 1) * NB] = t_ref[g, :NB]
    slots = 2 * devs
    row = lax.broadcasted_iota(jnp.int32, (slots, BLK), 0)
    inner = (row > 0) & (row < slots - 1)
    cell_ref[devs * NB :] = jnp.where(inner, group_ghosts(t_ref), -1.0)

    def chunk(c, _):
        here = pl.ds(pl.multiple_of(c * 8, 8), 8)

        def use(r, value):
            out_ref[r, here, :] = value

        solve_rows(cell_ref[here, :], inv, use)
        return 0

    lax.fori_loop(0, cell_ref.shape[0] // 8, chunk, 0, unroll=2)
    emit(0)


def spread(part, sums, part_ref):
    devs = part_ref.shape[0]
    part_ref[:, :NB, :] = part[: devs * NB].reshape(devs, NB, BLK)
    for g in range(devs):
        ghosts = part[devs * NB + 2 * g : devs * NB + 2 * g + 2]
        part_ref[g, NB:, :] = jnp.concatenate([ghosts, sums], axis=0)


def coarse_body(
    ready, emit, rows_hbm, diag_ref, g_ref, part_ref, wh_ref, wl_ref, rows_ref, sh_ref, sl_ref, oh_ref, sem
):
    copy = pltpu.make_async_copy(rows_hbm, rows_ref, sem)
    copy.start()
    devs = g_ref.shape[0]
    sources = devs * NB
    cells = g_ref[:, NB : NB + 1, :].reshape(devs, BLK)
    cells = jnp.sum(cells.reshape(devs // 8, 8, BLK), axis=1)
    sub = lax.broadcasted_iota(jnp.int32, (BLK, BLK), 0)
    for r in range(CROWS):
        index = (sub + r * BLK).astype(F32)
        for q in range(devs // 8):
            hit = jnp.where(cells[q : q + 1] == index, 1.0, 0.0)
            oh_ref[r * BLK : (r + 1) * BLK, q * BLK : (q + 1) * BLK] = hit.astype(BF16)
    place = lax.axis_index(GATHER)
    before = g_ref[(place + devs - 1) % devs][NB + 1 : NB + 2]
    after = g_ref[(place + 1) % devs][NB + 2 : NB + 3]
    row = lax.broadcasted_iota(jnp.int32, (8, BLK), 0)
    outer = jnp.where(row == 0, before, jnp.where(row == 7, after, -1.0))
    copy.wait()
    size = rows_ref.shape[1]
    base = size - NB

    def use(r, value):
        rows_ref[r, base : base + 8, :] += jnp.where(row == 0, value, 0.0)
        rows_ref[r, size - 8 :, :] += jnp.where(row == 7, value, 0.0)

    solve_rows(outer, 1.0 / (4.0 + diag_ref[...]), use)
    for r in range(CROWS):
        here = slice(r * BLK, (r + 1) * BLK)
        high, low = split(rows_ref[r])
        sh_ref[:, here] = high
        sl_ref[:, here] = low
    w = dot(sh_ref[...], oh_ref[...]) + dot(sl_ref[...], oh_ref[...])
    wh, wl = split(w)
    wh_ref[...] = wh
    wl_ref[...] = wl
    emit(1)
    emit(2)
    gh, gl = split(g_ref[:, :NB, :].reshape(sources, BLK))
    part = dot(wh, gh) + (dot(wh, gl) + dot(wl, gh))
    spread(part, jnp.zeros((ROWS - EXT, BLK), F32), part_ref)
    emit(0)


def apply_body(ready, emit, wh_ref, wl_ref, g_ref, part_ref):
    devs = g_ref.shape[0]
    gh, gl = split(g_ref[:, :NB, :].reshape(devs * NB, BLK))
    wh = wh_ref[...]
    part = dot(wh, gh) + (dot(wh, gl) + dot(wl_ref[...], gh))
    sums = jnp.sum(g_ref[:, NB:, :], axis=0)
    pad = jnp.zeros((ROWS - EXT - (MROWS - NB), BLK), F32)
    spread(part, jnp.concatenate([sums, pad], axis=0), part_ref)
    emit(0)


def operator_kernel(first, cols_hbm, s_hbm, f_hbm, inner_hbm, outer_hbm, *rest):
    if first:
        (w_hbm, out_hbm, q_hbm, cols_ref, s_ref, f_ref, inner_ref, outer_ref, out_ref, xh, sem, out_sem,
         w_ref, q_ref, xl) = rest
    else:
        out_hbm, cols_ref, s_ref, f_ref, inner_ref, outer_ref, out_ref, xh, sem, out_sem = rest
    steps = NB // GROUP

    def part(ref, g):
        return ref.at[pl.ds(g * GROUP, GROUP)]

    def block(g):
        return pltpu.make_async_copy(part(s_hbm, g), part(s_ref, g), sem.at[g])

    def result(n, g):
        source, target = ((out_ref, out_hbm), (q_ref, q_hbm))[n] if first else (out_ref, out_hbm)
        return pltpu.make_async_copy(part(source, g), part(target, g), out_sem.at[n, g])

    pairs = [(cols_hbm, cols_ref), (f_hbm, f_ref), (inner_hbm, inner_ref), (outer_hbm, outer_ref)]
    if first:
        pairs.append((w_hbm, w_ref))
    head = [pltpu.make_async_copy(a, b, sem.at[steps + n]) for n, (a, b) in enumerate(pairs)]
    for copy in head:
        copy.start()
    for g in range(steps):
        block(g).start()
    for copy in head:
        copy.wait()
    lane = lax.broadcasted_iota(jnp.int32, (BLK, BLK), 1)
    odd = lax.axis_index("crs") % 2 == 1

    def lower(rows):
        return jnp.where(odd, inner_ref[rows, :], outer_ref[rows, :])

    def upper(rows):
        return jnp.where(odd, outer_ref[rows, :], inner_ref[rows, :])

    if first:
        wt = w_ref[...].T
        turned = jnp.concatenate([lower(slice(BLK, None)), upper(slice(BLK, None))], axis=0).T
    for e in range(EXT):
        x = f_ref[e] if e < NB else (lower, upper)[e - NB](slice(0, BLK))
        high, low = split(x)
        xh[e, :, :BLK] = high
        if first:
            xl[e, :, :BLK] = low
            at = 8 * (e - NB)
            col = wt[:, e : e + 1] if e < NB else turned[:, at : at + 1]
            high, low = split(jnp.where((lane % 32 == e) & (lane < 96), col, 0.0))
            xh[e, :, BLK:] = high
            xl[e, :, BLK:] = low
        else:
            xh[e, :, BLK:] = low

    def step(g, _):
        block(g).wait()
        for b in range(GROUP):
            i = g * GROUP + b
            sh, sl, vh, vl = [], [], [], []
            for k in range(KB):
                col = cols_ref[k, i]
                high, low = split(s_ref[i, k])
                sh.append(high)
                sl.append(low)
                vh.append(xh[col])
                if first:
                    vl.append(xl[col])
            sh = jnp.concatenate(sh, axis=1)
            both = jnp.concatenate([sh, jnp.concatenate(sl, axis=1)], axis=0)
            image = dot(both, jnp.concatenate(vh, axis=0))
            if first:
                image = image[:BLK] + (image[BLK:] + dot(sh, jnp.concatenate(vl, axis=0)))
                high, low = split(image[:, BLK:])
                q_ref[i] = jnp.where((lane >= 32) & (lane < 64), low.astype(F32), high.astype(F32)).astype(BF16)
                image = image[:, :BLK]
            else:
                image = image[:BLK, :BLK] + (image[:BLK, BLK:] + image[BLK:, :BLK])
            out_ref[i] = image
        result(0, g).start()
        if first:
            result(1, g).start()
        return 0

    lax.fori_loop(0, steps, step, 0)
    for g in range(steps):
        result(0, g).wait()
        if first:
            result(1, g).wait()


def pack(u):
    keep = lax.broadcasted_iota(jnp.int32, (ROWS, BLK), 0) < EXT
    u = jnp.concatenate([jnp.where(keep, u, 0.0), jnp.zeros((32 - ROWS, BLK), F32)], axis=0)
    high, low = split(u)
    return jnp.concatenate([high, high, low, jnp.zeros((32, BLK), BF16)], axis=0)


def fold(x):
    return jnp.sum(x.reshape(BLK // 8, 8, BLK), axis=0)


def message(rows, dots):
    sums = [jnp.sum(d, axis=0, keepdims=True) for d in dots]
    pad = [jnp.zeros((1, BLK), F32)] * (MROWS - NB - len(dots))
    return jnp.concatenate(rows + sums + pad, axis=0)


def first_body(ready, emit, got_ref, w_ref, r_ref, dr_ref, adr_ref, q_ref, msg_ref, u_ref, im_ref):
    u = jnp.sum(got_ref[...], axis=0)
    u_ref[...] = u
    emit(1)
    packed = pack(u)
    wt = w_ref[...].T
    rows = []
    rz = jnp.zeros((8, BLK), F32)
    zw = jnp.zeros((8, BLK), F32)
    for c, blocks in chunks():
        ready(c)
        for i in blocks:
            col = wt[:, i : i + 1]
            image = adr_ref[i] + dot(q_ref[i], packed)
            z = dr_ref[i] + col * u[i : i + 1]
            im_ref[i] = image
            rows.append(jnp.sum(col * image, axis=0, keepdims=True))
            rz = rz + fold(r_ref[i] * z)
            zw = zw + fold(z * image)
        emit(2, c)
    broadcast(msg_ref, message(rows, [rz, zw]))
    emit(0)


def second_body(
    ready, emit, got_ref, u_ref, w_ref, r_ref, im_ref, dr_ref, dim_ref, adr_ref, adim_ref, q_ref,
    msg_ref, v_ref, az_ref,
):
    v = jnp.sum(got_ref[...], axis=0)
    v_ref[...] = v
    emit(1)
    alpha = v[EXT : EXT + 1] / v[EXT + 1 : EXT + 2]
    u0 = u_ref[...]
    u = u0 - alpha * v
    packed = pack(u)
    wt = w_ref[...].T
    rows = []
    rz = jnp.zeros((8, BLK), F32)
    zaz = jnp.zeros((8, BLK), F32)
    cross = jnp.zeros((8, BLK), F32)
    for c, blocks in chunks():
        ready(c)
        for i in blocks:
            col = wt[:, i : i + 1]
            image = im_ref[i]
            dr = dr_ref[i]
            z0 = dr + col * u0[i : i + 1]
            z1 = dr - alpha * dim_ref[i] + col * u[i : i + 1]
            az = adr_ref[i] - alpha * adim_ref[i] + dot(q_ref[i], packed)
            az_ref[i] = az
            rows.append(jnp.sum(col * az, axis=0, keepdims=True))
            rz = rz + fold((r_ref[i] - alpha * image) * z1)
            zaz = zaz + fold(z1 * az)
            cross = cross + fold(z1 * image + z0 * az)
        emit(2, c)
    broadcast(msg_ref, message(rows, [rz, zaz, cross]))
    emit(0)


def last_body(
    ready, emit, got_ref, u_ref, v_ref, w_ref, r_ref, im_ref, dr_ref, dim_ref, az_ref, daz_ref,
    sol_ref, res_ref, pre_ref,
):
    t = jnp.sum(got_ref[...], axis=0)
    v = v_ref[...]
    gamma0 = v[EXT : EXT + 1]
    curve0 = v[EXT + 1 : EXT + 2]
    gamma1 = t[EXT : EXT + 1]
    alpha0 = gamma0 / curve0
    beta = gamma1 / gamma0
    curve1 = t[EXT + 1 : EXT + 2] + beta * (t[EXT + 2 : EXT + 3] + beta * curve0)
    alpha1 = gamma1 / curve1
    u0 = u_ref[...]
    u1 = u0 - alpha0 * v
    u2 = u1 - alpha1 * (t + beta * v)
    wt = w_ref[...].T
    for c, blocks in chunks():
        ready(c)
        for i in blocks:
            col = wt[:, i : i + 1]
            image = im_ref[i]
            dr = dr_ref[i]
            dim = dim_ref[i]
            z0 = dr + col * u0[i : i + 1]
            dr1 = dr - alpha0 * dim
            z1 = dr1 + col * u1[i : i + 1]
            sol_ref[i] = alpha0 * z0 + alpha1 * (z1 + beta * z0)
            res_ref[i] = r_ref[i] - alpha0 * image - alpha1 * (az_ref[i] + beta * image)
            local = dr1 - alpha1 * (daz_ref[i] + beta * dim)
            pre_ref[i] = local + col * u2[i : i + 1]
        for n in range(3):
            emit(n, c)


FIELD = (NB, BLK, BLK)


def apply_operator(stiffness, columns, field, inner, outer, weights=None):
    first = weights is not None
    hbm = pl.BlockSpec(memory_space=pltpu.HBM)
    outs = [jax.ShapeDtypeStruct(FIELD, F32)]
    args = [columns, stiffness, field, inner, outer]
    scratch = [
        pltpu.SMEM(columns.shape, jnp.int32),
        pltpu.VMEM(stiffness.shape, F32),
        pltpu.VMEM(FIELD, F32),
        pltpu.VMEM(inner.shape, F32),
        pltpu.VMEM(outer.shape, F32),
        pltpu.VMEM(FIELD, F32),
        pltpu.VMEM((EXT, BLK, 2 * BLK), BF16),
        pltpu.SemaphoreType.DMA((NB // GROUP + 5,)),
        pltpu.SemaphoreType.DMA((2, NB // GROUP)),
    ]
    if first:
        outs.append(jax.ShapeDtypeStruct(FIELD, BF16))
        args.append(weights)
        scratch += [
            pltpu.VMEM(weights.shape, F32),
            pltpu.VMEM(FIELD, BF16),
            pltpu.VMEM((EXT, BLK, 2 * BLK), BF16),
        ]
    return pl.pallas_call(
        functools.partial(operator_kernel, first),
        out_shape=outs,
        in_specs=[hbm] * len(args),
        out_specs=[hbm] * len(outs),
        scratch_shapes=scratch,
        compiler_params=pltpu.CompilerParams(vmem_limit_bytes=BIG),
        cost_estimate=pl.CostEstimate(flops=6 * 10**9, bytes_accessed=8 << 20, transcendentals=0),
    )(*args)


def on_device(
    loads, stiffness, inv_diag, columns, send_lists, restrict_weights, coarse_map, coarse_diag
):
    devices = lax.axis_size(RING)
    gathered = lax.axis_size(GATHER)
    scattered = lax.axis_size(SCATTER)
    swaps = []
    for first in (0, 1):
        pairs = [((first + 2 * i) % devices, (first + 2 * i + 1) % devices) for i in range(devices // 2)]
        swaps.append(pairs + [(j, i) for i, j in pairs])
    send = (send_lists.reshape(1, 2), "scalar")
    cells = (coarse_map, "scalar")
    columns = columns.T
    weights = (restrict_weights, "whole")
    msg_out = ((gathered, MROWS, BLK), F32, "whole")
    part_shape = (scattered, ROWS, BLK)
    part_out = (part_shape, F32, "whole")
    short_out = (part_shape[1:], F32, "whole")
    field_out = (FIELD, F32, "field")
    big = 2 << 20

    (target,) = staged(
        target_body,
        [send, cells],
        [((scattered, TROWS, BLK), F32, "whole")],
        moved=1 << 18,
    )
    targets = lax.all_to_all(target, SCATTER, 0, 0, tiled=True)
    (start_rows,) = staged(
        start_body,
        [cells, weights, (loads, "field")],
        [((ROWS, BLK), F32, "vmem")],
        flops=10**6,
        moved=big,
    )
    (msg,) = staged(
        open_body, [(start_rows, "vmem"), (targets, "vmem")], [msg_out], moved=1 << 18, limit=SMALL
    )
    got = lax.all_to_all(msg, GATHER, 0, 0, tiled=True)
    packet = ((BLK + 8, BLK), F32, "vmem")
    local, inner, outer = staged(
        local_body,
        [send, weights, (loads, "field"), (inv_diag, "field")],
        [field_out, packet, packet],
        flops=2 * 10**8,
        moved=big,
    )
    inner = lax.ppermute(inner, RING, swaps[0])
    outer = lax.ppermute(outer, RING, swaps[1])
    rows = scattered * EXT
    (coarse_rows,) = staged(
        sweep_body,
        [(targets, "vmem"), (coarse_diag, "vmem")],
        [((CROWS, rows, BLK), F32, "whole")],
        scratch=[pltpu.VMEM((rows, BLK), F32)],
        flops=10**8,
        moved=big,
        limit=SMALL,
    )
    got, inner, outer = lax.optimization_barrier((got, inner, outer))
    image_local, coupling = apply_operator(
        stiffness, columns, local, inner, outer, restrict_weights
    )
    weights_out = ((rows, gathered * NB), BF16, "whole")
    cells_all = CROWS * BLK
    part, wh, wl = staged(
        coarse_body,
        [(coarse_rows, "hbm"), (coarse_diag, "vmem"), (got, "vmem")],
        [part_out, weights_out, weights_out],
        scratch=[
            pltpu.VMEM((CROWS, rows, BLK), F32),
            pltpu.VMEM((rows, cells_all), BF16),
            pltpu.VMEM((rows, cells_all), BF16),
            pltpu.VMEM((cells_all, gathered * NB), BF16),
            pltpu.SemaphoreType.DMA(()),
        ],
        flops=10**9,
        moved=big,
        limit=SMALL,
    )
    got = lax.all_to_all(part, SCATTER, 0, 0, tiled=True)

    msg, u0, image0 = staged(
        first_body,
        [(got, "whole"), weights, (loads, "field"), (local, "field"), (image_local, "field"),
         (coupling, "field")],
        [msg_out, short_out, field_out],
        flops=10**8,
        moved=big,
    )
    packet = ((BLK, BLK), F32, "vmem")
    local_image, inner, outer = staged(
        image_body,
        [send, (image0, "field"), (inv_diag, "field")],
        [field_out, packet, packet],
        flops=2 * 10**8,
        moved=big,
    )
    inner = lax.ppermute(inner, RING, swaps[0])
    outer = lax.ppermute(outer, RING, swaps[1])
    (image_image,) = apply_operator(stiffness, columns, local_image, inner, outer)

    def exchange(msg, ahead):
        got = lax.all_to_all(msg, GATHER, 0, 0, tiled=True)
        got, ahead = lax.optimization_barrier((got, ahead))
        (part,) = staged(
            apply_body,
            [(wh, "whole"), (wl, "whole"), (got, "vmem")],
            [part_out],
            flops=10**8,
            moved=big,
            limit=SMALL,
        )
        return lax.all_to_all(part, SCATTER, 0, 0, tiled=True), ahead

    got, local_image = exchange(msg, local_image)
    msg, v0, image1 = staged(
        second_body,
        [(got, "whole"), (u0, "whole"), weights, (loads, "field"), (image0, "field"),
         (local, "field"), (local_image, "field"), (image_local, "field"),
         (image_image, "field"), (coupling, "field")],
        [msg_out, short_out, field_out],
        flops=10**8,
        moved=big,
    )
    (local_image1,) = staged(
        product_body,
        [(image1, "field"), (inv_diag, "field")],
        [field_out],
        flops=2 * 10**8,
        moved=big,
    )
    got, local_image1 = exchange(msg, local_image1)
    return tuple(
        staged(
            last_body,
            [(got, "whole"), (u0, "whole"), (v0, "whole"), weights, (loads, "field"),
             (image0, "field"), (local, "field"), (local_image, "field"), (image1, "field"),
             (local_image1, "field")],
            [field_out] * 3,
            flops=10**8,
            moved=big,
        )
    )


def solution(mesh):
    chips = mesh.devices.reshape(4, 8, 2, mesh.shape["crs"])
    fine = Mesh(chips, RING)
    placed = P(RING)
    return jax.shard_map(
        on_device,
        mesh=fine,
        in_specs=(placed,) * 7 + (P(),),
        out_specs=(placed,) * 3,
        check_vma=False,
    )
```

```python
import functools

import jax
import jax.numpy as jnp
from jax import lax
from jax.experimental import pallas as pl
from jax.experimental.pallas import tpu as pltpu
from jax.sharding import Mesh, PartitionSpec as P

OMEGA = 0.8
SWEEPS = 4
NB = 16
BLK = 128
KB = 6
EXT = 18
DOTS = EXT
ROWS = 24
CROWS = 16
RING = ("y", "z", "core", "crs")
GATHER = ("y", "z")
SCATTER = ("core", "crs")
F32 = jnp.float32
BF16 = jnp.bfloat16
BIG = 60 * 1024 * 1024
SMALL = 12 * 1024 * 1024
TROWS = 48
GROUP = 4
CHUNK = 8


def sweep_coefficients():
    total = [0.0] * SWEEPS
    power = [1.0]
    for _ in range(SWEEPS):
        for i, c in enumerate(power):
            total[i] += c
        grown = [0.0] * (len(power) + 1)
        for i, c in enumerate(power):
            grown[i] += c * (1.0 - OMEGA)
            grown[i + 1] += c * OMEGA
        power = grown
    return total


def split(x):
    high = x.astype(BF16)
    return high, (x - high.astype(F32)).astype(BF16)


def dot(a, b):
    return jnp.dot(a, b, preferred_element_type=F32)


def dot3(a, b):
    ah, al = split(a)
    bh, bl = split(b)
    return dot(ah, bh) + (dot(ah, bl) + dot(al, bh))


def staged(body, ins, outs, scratch=(), flops=0, moved=0, limit=BIG):
    kinds_in = [k for _, k in ins]
    kinds_out = [k for _, _, k in outs]
    n_in, n_out = len(ins), len(outs)
    parts = NB // CHUNK

    def buffer(shape, dtype, kind):
        return pltpu.SMEM(shape, dtype) if kind == "scalar" else pltpu.VMEM(shape, dtype)

    buffers = [buffer(a.shape, a.dtype, k) for a, k in ins if k not in ("vmem", "hbm")]
    buffers += [buffer(sh, dt, k) for sh, dt, k in outs if k != "vmem"]

    def kernel(*refs):
        sources, targets = refs[:n_in], refs[n_in : n_in + n_out]
        rest = list(refs[n_in + n_out :])
        sem_in, sem_out = rest.pop(), rest.pop()
        bufs_in = [r if k in ("vmem", "hbm") else rest.pop(0) for r, k in zip(sources, kinds_in)]
        bufs_out = [r if k == "vmem" else rest.pop(0) for r, k in zip(targets, kinds_out)]

        def chunk(ref, c):
            return ref.at[pl.ds(c * CHUNK, CHUNK)]

        first = [
            pltpu.make_async_copy(s, b, sem_in.at[j, 0])
            for j, (s, b, k) in enumerate(zip(sources, bufs_in, kinds_in))
            if k in ("whole", "scalar", "any")
        ]
        fields = [
            [
                pltpu.make_async_copy(chunk(s, c), chunk(b, c), sem_in.at[j, c])
                for j, (s, b, k) in enumerate(zip(sources, bufs_in, kinds_in))
                if k == "field"
            ]
            for c in range(parts)
        ]
        for copy in first + sum(fields, []):
            copy.start()
        sent = []

        def ready(c):
            for copy in fields[c]:
                copy.wait()

        def emit(n, c=0):
            if kinds_out[n] == "field":
                copy = pltpu.make_async_copy(chunk(bufs_out[n], c), chunk(targets[n], c), sem_out.at[n, c])
            else:
                copy = pltpu.make_async_copy(bufs_out[n], targets[n], sem_out.at[n, 0])
            copy.start()
            sent.append(copy)

        for copy in first:
            copy.wait()
        body(ready, emit, *bufs_in, *bufs_out, *rest)
        for copy in sent:
            copy.wait()

    def spec(kind):
        return pl.BlockSpec(memory_space={"vmem": pltpu.VMEM, "any": pl.ANY}.get(kind, pltpu.HBM))

    return pl.pallas_call(
        kernel,
        out_shape=[jax.ShapeDtypeStruct(sh, dt) for sh, dt, _ in outs],
        in_specs=[spec(k) for k in kinds_in],
        out_specs=[spec(k) for k in kinds_out],
        scratch_shapes=buffers
        + list(scratch)
        + [pltpu.SemaphoreType.DMA((n_out, parts)), pltpu.SemaphoreType.DMA((n_in, parts))],
        compiler_params=pltpu.CompilerParams(vmem_limit_bytes=limit),
        cost_estimate=pl.CostEstimate(flops=flops, bytes_accessed=moved, transcendentals=0),
    )(*[a for a, _ in ins])


def column_cells(map_ref):
    rows = [jnp.full((1, BLK), map_ref[i], jnp.int32) for i in range(NB)]
    return jnp.concatenate(rows, axis=0).astype(F32)


def broadcast(msg_ref, rows):
    for a in range(msg_ref.shape[0]):
        msg_ref[a] = rows


def chunks():
    return [(c, range(c * CHUNK, (c + 1) * CHUNK)) for c in range(NB // CHUNK)]


def start_body(ready, emit, map_ref, w_ref, r_ref, rows_ref):
    wt = w_ref[...].T
    lane = lax.broadcasted_iota(jnp.int32, (1, BLK), 1)
    cells = jnp.zeros((1, BLK), jnp.int32)
    for i in range(NB):
        cells = jnp.where(lane % NB == i, map_ref[i], cells)
    mine = lane // NB == lax.axis_index(GATHER) % 8
    cells = jnp.where(mine, cells, 0).astype(F32)
    rows = []
    for c, blocks in chunks():
        ready(c)
        rows += [jnp.sum(wt[:, i : i + 1] * r_ref[i], axis=0, keepdims=True) for i in blocks]
    rows_ref[...] = jnp.concatenate(rows + [cells, jnp.zeros((ROWS - NB - 1, BLK), F32)], axis=0)


def group_ghosts(t_ref):
    return jnp.sum(t_ref[:, NB : 2 * NB, :], axis=0)


def open_body(ready, emit, rows_ref, t_ref, msg_ref):
    ghosts = group_ghosts(t_ref)
    lane = lax.broadcasted_iota(jnp.int32, (1, BLK), 1)
    ends = jnp.where(lane < BLK // 2, ghosts[:1], ghosts[NB - 1 :])
    rows = jnp.concatenate([rows_ref[: NB + 1], ends], axis=0)
    broadcast(msg_ref, rows)
    emit(0)


def slot_of(swap):
    return (lax.axis_index("crs") + 1 + swap) % 2


def local_body(ready, emit, send_ref, w_ref, r_ref, d_ref, out_ref, inner_ref, outer_ref, dot_ref):
    total = jnp.zeros((8, BLK), F32)
    for c, blocks in chunks():
        ready(c)
        for i in blocks:
            product = dot3(d_ref[i], r_ref[i])
            out_ref[i] = product
            total = total + fold(r_ref[i] * product)
        emit(0, c)
    dot_ref[...] = total
    emit(3)
    for n, ref in ((0, inner_ref), (1, outer_ref)):
        block = send_ref[0, slot_of(n)]
        ref[:BLK] = out_ref[block]
        ref[BLK:] = jnp.concatenate(
            [w_ref[pl.ds(block, 1), :], jnp.zeros((7, BLK), F32)], axis=0
        )


def target_body(ready, emit, send_ref, map_ref, diag_ref, out_ref):
    slots = 2 * out_ref.shape[0]
    place = lax.axis_index(SCATTER)
    row = lax.broadcasted_iota(jnp.int32, (slots, BLK), 0)
    to_next = jnp.full((slots, BLK), map_ref[send_ref[0, 1]], jnp.int32)
    to_prev = jnp.full((slots, BLK), map_ref[send_ref[0, 0]], jnp.int32)
    ghosts = jnp.where(row == (2 * place + 2) % slots, to_next, 0)
    ghosts = jnp.where(row == (2 * place + slots - 1) % slots, to_prev, ghosts).astype(F32)
    own = column_cells(map_ref)
    for a in range(out_ref.shape[0]):
        out_ref[a, :NB] = own
        out_ref[a, NB : 2 * NB] = ghosts
        out_ref[a, 2 * NB :] = diag_ref[...]
    emit(0)


def image_body(
    ready, emit, send_ref, u_ref, adr_ref, q_ref, d_ref, im_ref, out_ref, inner_ref, outer_ref
):
    packed = pack(u_ref[...])
    for c, blocks in chunks():
        ready(c)
        for i in blocks:
            image = adr_ref[i] + dot(q_ref[i], packed)
            im_ref[i] = image
            out_ref[i] = dot3(d_ref[i], image)
        emit(0, c)
        emit(1, c)
    for n, ref in ((0, inner_ref), (1, outer_ref)):
        ref[...] = out_ref[send_ref[0, slot_of(n)]]


def product_body(ready, emit, v_ref, im_ref, adim_ref, q_ref, d_ref, az_ref, daz_ref):
    v = v_ref[...]
    alpha = v[EXT : EXT + 1] / v[EXT + 1 : EXT + 2]
    packed = pack(v)
    for c, blocks in chunks():
        ready(c)
        for i in blocks:
            az = im_ref[i] - alpha * (adim_ref[i] + dot(q_ref[i], packed))
            az_ref[i] = az
            daz_ref[i] = dot3(d_ref[i], az)
        emit(0, c)
        emit(1, c)


def solve_rows(cell, inv, use):
    coef = sweep_coefficients()
    lane = lax.broadcasted_iota(jnp.int32, (8, BLK), 1)
    spot = [jnp.where(cell == (lane + BLK * r).astype(F32), 1.0, 0.0) for r in range(CROWS)]
    t = [coef[-1] * spot[r] for r in range(CROWS)]
    for power in range(SWEEPS - 2, -1, -1):
        y = [t[r] * inv[r : r + 1] for r in range(CROWS)]
        new = []
        for r in range(CROWS):
            v = jnp.where(lane == 0, 0.0, pltpu.roll(y[r], 1, 1))
            v = v + jnp.where(lane == BLK - 1, 0.0, pltpu.roll(y[r], BLK - 1, 1))
            if r > 0:
                v = v + y[r - 1]
            if r < CROWS - 1:
                v = v + y[r + 1]
            new.append(v + coef[power] * spot[r])
        t = new
    for r in range(CROWS):
        use(r, t[r] * (inv[r : r + 1] * OMEGA))


def sweep_body(ready, emit, t_ref, out_ref, cell_ref):
    inv = 1.0 / (4.0 + t_ref[0, 2 * NB :, :])
    out_ref[CROWS, :CROWS, :] = inv
    devs = t_ref.shape[0]
    for g in range(devs):
        cell_ref[g * NB : (g + 1) * NB] = t_ref[g, :NB]
    slots = 2 * devs
    row = lax.broadcasted_iota(jnp.int32, (slots, BLK), 0)
    inner = (row > 0) & (row < slots - 1)
    cell_ref[devs * NB :] = jnp.where(inner, group_ghosts(t_ref), -1.0)

    def chunk(c, _):
        here = pl.ds(pl.multiple_of(c * 8, 8), 8)

        def use(r, value):
            out_ref[r, here, :] = value

        solve_rows(cell_ref[here, :], inv, use)
        return 0

    lax.fori_loop(0, cell_ref.shape[0] // 8, chunk, 0, unroll=3)
    emit(0)


def spread(part, sums, part_ref):
    devs = part_ref.shape[0]
    part_ref[:, :NB, :] = part[: devs * NB].reshape(devs, NB, BLK)
    for g in range(devs):
        ghosts = part[devs * NB + 2 * g : devs * NB + 2 * g + 2]
        part_ref[g, NB:, :] = jnp.concatenate([ghosts, sums], axis=0)


def coarse_body(
    ready, emit, rows_hbm, g_ref, part_ref, wh_ref, wl_ref, rows_ref, sh_ref, sl_ref, oh_ref, sem
):
    copy = pltpu.make_async_copy(rows_hbm, rows_ref, sem)
    copy.start()
    devs = g_ref.shape[0]
    sources = devs * NB
    cells = g_ref[:, NB : NB + 1, :].reshape(devs, BLK)
    cells = jnp.sum(cells.reshape(devs // 8, 8, BLK), axis=1)
    sub = lax.broadcasted_iota(jnp.int32, (BLK, BLK), 0)
    for r in range(CROWS):
        index = (sub + r * BLK).astype(F32)
        for q in range(devs // 8):
            hit = jnp.where(cells[q : q + 1] == index, 1.0, 0.0)
            oh_ref[r * BLK : (r + 1) * BLK, q * BLK : (q + 1) * BLK] = hit.astype(BF16)
    place = lax.axis_index(GATHER)
    before = g_ref[(place + devs - 1) % devs][NB + 1 : NB + 2, :1]
    after = g_ref[(place + 1) % devs][NB + 1 : NB + 2, BLK - 1 :]
    row = lax.broadcasted_iota(jnp.int32, (8, BLK), 0)
    outer = jnp.where(row == 0, before, jnp.where(row == 7, after, -1.0))
    copy.wait()
    size = rows_ref.shape[1]
    base = size - NB

    def use(r, value):
        rows_ref[r, base : base + 8, :] += jnp.where(row == 0, value, 0.0)
        rows_ref[r, size - 8 :, :] += jnp.where(row == 7, value, 0.0)

    solve_rows(outer, rows_ref[CROWS, :CROWS, :], use)
    for r in range(CROWS):
        here = slice(r * BLK, (r + 1) * BLK)
        high, low = split(rows_ref[r])
        sh_ref[:, here] = high
        sl_ref[:, here] = low
    w = dot(sh_ref[...], oh_ref[...]) + dot(sl_ref[...], oh_ref[...])
    wh, wl = split(w)
    wh_ref[...] = wh
    wl_ref[...] = wl
    emit(1)
    emit(2)
    gh, gl = split(g_ref[:, :NB, :].reshape(sources, BLK))
    part = dot(wh, gh) + (dot(wh, gl) + dot(wl, gh))
    spread(part, jnp.zeros((ROWS - EXT, BLK), F32), part_ref)
    emit(0)


def apply_body(ready, emit, wh_ref, wl_ref, g_ref, part_ref):
    devs = g_ref.shape[0]
    gh, gl = split(g_ref[:, :NB, :].reshape(devs * NB, BLK))
    wh = wh_ref[...]
    part = dot(wh, gh) + (dot(wh, gl) + dot(wl_ref[...], gh))
    sums = jnp.sum(g_ref[:, NB:, :], axis=0)
    pad = jnp.zeros((ROWS - DOTS - sums.shape[0], BLK), F32)
    spread(part, jnp.concatenate([sums, pad], axis=0), part_ref)
    emit(0)


def operator_kernel(first, cols_hbm, s_hbm, f_hbm, inner_hbm, outer_hbm, *rest):
    if first:
        (w_hbm, out_hbm, q_hbm, cols_ref, s_ref, f_ref, inner_ref, outer_ref, out_ref, xh, sem, out_sem,
         w_ref, q_ref, xl) = rest
    else:
        out_hbm, cols_ref, s_ref, f_ref, inner_ref, outer_ref, out_ref, xh, sem, out_sem = rest
    steps = NB // GROUP

    def part(ref, g):
        return ref.at[pl.ds(g * GROUP, GROUP)]

    def block(g):
        return pltpu.make_async_copy(part(s_hbm, g), part(s_ref, g), sem.at[g])

    def result(n, g):
        source, target = ((out_ref, out_hbm), (q_ref, q_hbm))[n] if first else (out_ref, out_hbm)
        return pltpu.make_async_copy(part(source, g), part(target, g), out_sem.at[n, g])

    pairs = [(cols_hbm, cols_ref), (f_hbm, f_ref), (inner_hbm, inner_ref), (outer_hbm, outer_ref)]
    if first:
        pairs.append((w_hbm, w_ref))
    head = [pltpu.make_async_copy(a, b, sem.at[steps + n]) for n, (a, b) in enumerate(pairs)]
    for copy in head:
        copy.start()
    for g in range(steps):
        block(g).start()
    for copy in head:
        copy.wait()
    lane = lax.broadcasted_iota(jnp.int32, (BLK, BLK), 1)
    odd = lax.axis_index("crs") % 2 == 1

    def lower(rows):
        return jnp.where(odd, inner_ref[rows, :], outer_ref[rows, :])

    def upper(rows):
        return jnp.where(odd, outer_ref[rows, :], inner_ref[rows, :])

    if first:
        wt = w_ref[...].T
        turned = jnp.concatenate([lower(slice(BLK, None)), upper(slice(BLK, None))], axis=0).T
    for e in range(EXT):
        x = f_ref[e] if e < NB else (lower, upper)[e - NB](slice(0, BLK))
        high, low = split(x)
        xh[e, :, :BLK] = high
        if first:
            xl[e, :, :BLK] = low
            at = 8 * (e - NB)
            col = wt[:, e : e + 1] if e < NB else turned[:, at : at + 1]
            high, low = split(jnp.where((lane % 32 == e) & (lane < 96), col, 0.0))
            xh[e, :, BLK:] = high
            xl[e, :, BLK:] = low
        else:
            xh[e, :, BLK:] = low

    def step(g, _):
        block(g).wait()
        for b in range(GROUP):
            i = g * GROUP + b
            sh, sl, vh, vl = [], [], [], []
            for k in range(KB):
                col = cols_ref[k, i]
                high, low = split(s_ref[i, k])
                sh.append(high)
                sl.append(low)
                vh.append(xh[col])
                if first:
                    vl.append(xl[col])
            sh = jnp.concatenate(sh, axis=1)
            both = jnp.concatenate([sh, jnp.concatenate(sl, axis=1)], axis=0)
            image = dot(both, jnp.concatenate(vh, axis=0))
            if first:
                image = image[:BLK] + (image[BLK:] + dot(sh, jnp.concatenate(vl, axis=0)))
                high, low = split(image[:, BLK:])
                q_ref[i] = jnp.where((lane >= 32) & (lane < 64), low.astype(F32), high.astype(F32)).astype(BF16)
                image = image[:, :BLK]
            else:
                image = image[:BLK, :BLK] + (image[:BLK, BLK:] + image[BLK:, :BLK])
            out_ref[i] = image
        result(0, g).start()
        if first:
            result(1, g).start()
        return 0

    lax.fori_loop(0, steps, step, 0)
    for g in range(steps):
        result(0, g).wait()
        if first:
            result(1, g).wait()


def pack(u):
    keep = lax.broadcasted_iota(jnp.int32, (ROWS, BLK), 0) < EXT
    u = jnp.concatenate([jnp.where(keep, u, 0.0), jnp.zeros((32 - ROWS, BLK), F32)], axis=0)
    high, low = split(u)
    return jnp.concatenate([high, high, low, jnp.zeros((32, BLK), BF16)], axis=0)


def fold_rows(x):
    return jnp.sum(x.reshape(NB // 8, 8, BLK), axis=0)


def fold(x):
    return jnp.sum(x.reshape(BLK // 8, 8, BLK), axis=0)


def message(rows, dots):
    sums = [jnp.sum(d, axis=0, keepdims=True) for d in dots]
    return jnp.concatenate(rows + sums, axis=0)


def first_body(
    ready, emit, got_ref, w_ref, rows_ref, dot_ref, dr_ref, adr_ref, q_ref, msg_ref, u_ref
):
    u = jnp.sum(got_ref[...], axis=0)
    u_ref[...] = u
    emit(1)
    packed = pack(u)
    wt = w_ref[...].T
    rows = []
    rz = dot_ref[...] + fold_rows(rows_ref[:NB] * u[:NB])
    zw = jnp.zeros((8, BLK), F32)
    for c, blocks in chunks():
        ready(c)
        for i in blocks:
            col = wt[:, i : i + 1]
            image = adr_ref[i] + dot(q_ref[i], packed)
            rows.append(jnp.sum(col * image, axis=0, keepdims=True))
            zw = zw + fold((dr_ref[i] + col * u[i : i + 1]) * image)
    broadcast(msg_ref, message(rows, [rz, zw]))
    emit(0)


def second_body(
    ready, emit, got_ref, u_ref, w_ref, r_ref, im_ref, dr_ref, dim_ref, adim_ref, q_ref,
    msg_ref, v_ref,
):
    v = jnp.sum(got_ref[...], axis=0)
    v_ref[...] = v
    emit(1)
    alpha = v[EXT : EXT + 1] / v[EXT + 1 : EXT + 2]
    u0 = u_ref[...]
    u1 = u0 - alpha * v
    packed = pack(v)
    wt = w_ref[...].T
    rows = []
    rz = jnp.zeros((8, BLK), F32)
    zaz = jnp.zeros((8, BLK), F32)
    cross = jnp.zeros((8, BLK), F32)
    for c, blocks in chunks():
        ready(c)
        for i in blocks:
            col = wt[:, i : i + 1]
            image = im_ref[i]
            dr = dr_ref[i]
            z0 = dr + col * u0[i : i + 1]
            z1 = dr - alpha * dim_ref[i] + col * u1[i : i + 1]
            az = image - alpha * (adim_ref[i] + dot(q_ref[i], packed))
            rows.append(jnp.sum(col * az, axis=0, keepdims=True))
            rz = rz + fold((r_ref[i] - alpha * image) * z1)
            zaz = zaz + fold(z1 * az)
            cross = cross + fold(z1 * image + z0 * az)
    broadcast(msg_ref, message(rows, [rz, zaz, cross]))
    emit(0)


def last_body(
    ready, emit, got_ref, u_ref, v_ref, w_ref, r_ref, im_ref, dr_ref, dim_ref, az_ref, daz_ref,
    sol_ref, res_ref, pre_ref,
):
    t = jnp.sum(got_ref[...], axis=0)
    v = v_ref[...]
    gamma0 = v[EXT : EXT + 1]
    curve0 = v[EXT + 1 : EXT + 2]
    gamma1 = t[EXT : EXT + 1]
    alpha0 = gamma0 / curve0
    beta = gamma1 / gamma0
    curve1 = t[EXT + 1 : EXT + 2] + beta * (t[EXT + 2 : EXT + 3] + beta * curve0)
    alpha1 = gamma1 / curve1
    u0 = u_ref[...]
    u1 = u0 - alpha0 * v
    u2 = u1 - alpha1 * (t + beta * v)
    wt = w_ref[...].T
    for c, blocks in chunks():
        ready(c)
        for i in blocks:
            col = wt[:, i : i + 1]
            image = im_ref[i]
            dr = dr_ref[i]
            dim = dim_ref[i]
            z0 = dr + col * u0[i : i + 1]
            dr1 = dr - alpha0 * dim
            z1 = dr1 + col * u1[i : i + 1]
            sol_ref[i] = alpha0 * z0 + alpha1 * (z1 + beta * z0)
            res_ref[i] = r_ref[i] - alpha0 * image - alpha1 * (az_ref[i] + beta * image)
            local = dr1 - alpha1 * (daz_ref[i] + beta * dim)
            pre_ref[i] = local + col * u2[i : i + 1]
        for n in range(3):
            emit(n, c)


FIELD = (NB, BLK, BLK)


def apply_operator(stiffness, columns, field, inner, outer, weights=None):
    first = weights is not None
    hbm = pl.BlockSpec(memory_space=pltpu.HBM)
    outs = [jax.ShapeDtypeStruct(FIELD, F32)]
    args = [columns, stiffness, field, inner, outer]
    scratch = [
        pltpu.SMEM(columns.shape, jnp.int32),
        pltpu.VMEM(stiffness.shape, F32),
        pltpu.VMEM(FIELD, F32),
        pltpu.VMEM(inner.shape, F32),
        pltpu.VMEM(outer.shape, F32),
        pltpu.VMEM(FIELD, F32),
        pltpu.VMEM((EXT, BLK, 2 * BLK), BF16),
        pltpu.SemaphoreType.DMA((NB // GROUP + 5,)),
        pltpu.SemaphoreType.DMA((2, NB // GROUP)),
    ]
    if first:
        outs.append(jax.ShapeDtypeStruct(FIELD, BF16))
        args.append(weights)
        scratch += [
            pltpu.VMEM(weights.shape, F32),
            pltpu.VMEM(FIELD, BF16),
            pltpu.VMEM((EXT, BLK, 2 * BLK), BF16),
        ]
    return pl.pallas_call(
        functools.partial(operator_kernel, first),
        out_shape=outs,
        in_specs=[hbm] * 3 + [pl.BlockSpec(memory_space=pl.ANY)] * 2 + [hbm] * (len(args) - 5),
        out_specs=[hbm] * len(outs),
        scratch_shapes=scratch,
        compiler_params=pltpu.CompilerParams(vmem_limit_bytes=BIG),
        cost_estimate=pl.CostEstimate(flops=6 * 10**9, bytes_accessed=8 << 20, transcendentals=0),
    )(*args)


def on_device(
    loads, stiffness, inv_diag, columns, send_lists, restrict_weights, coarse_map, coarse_diag
):
    devices = lax.axis_size(RING)
    gathered = lax.axis_size(GATHER)
    scattered = lax.axis_size(SCATTER)
    swaps = []
    for first in (0, 1):
        pairs = [((first + 2 * i) % devices, (first + 2 * i + 1) % devices) for i in range(devices // 2)]
        swaps.append(pairs + [(j, i) for i, j in pairs])
    send = (send_lists.reshape(1, 2), "scalar")
    cells = (coarse_map, "scalar")
    columns = columns.T
    weights = (restrict_weights, "whole")

    def msg_out(extra):
        return ((gathered, NB + extra, BLK), F32, "whole")

    part_shape = (scattered, ROWS, BLK)
    part_out = (part_shape, F32, "whole")
    short_out = (part_shape[1:], F32, "whole")
    field_out = (FIELD, F32, "field")
    big = 2 << 20

    (target,) = staged(
        target_body,
        [send, cells, (coarse_diag, "whole")],
        [((scattered, TROWS, BLK), F32, "whole")],
        moved=1 << 18,
    )
    targets = lax.all_to_all(target, SCATTER, 0, 0, tiled=True)
    (start_rows,) = staged(
        start_body,
        [cells, weights, (loads, "field")],
        [((ROWS, BLK), F32, "vmem")],
        flops=10**6,
        moved=big,
    )
    (msg,) = staged(
        open_body, [(start_rows, "vmem"), (targets, "vmem")], [msg_out(2)], moved=1 << 18, limit=SMALL
    )
    got = lax.all_to_all(msg, GATHER, 0, 0, tiled=True)
    packet = ((BLK + 8, BLK), F32, "vmem")
    local, inner, outer, local_dot = staged(
        local_body,
        [send, weights, (loads, "field"), (inv_diag, "field")],
        [field_out, packet, packet, ((8, BLK), F32, "whole")],
        flops=2 * 10**8,
        moved=big,
    )
    inner = lax.ppermute(inner, RING, swaps[0])
    outer = lax.ppermute(outer, RING, swaps[1])
    rows = scattered * EXT
    (coarse_rows,) = staged(
        sweep_body,
        [(targets, "vmem")],
        [((CROWS + 1, rows, BLK), F32, "whole")],
        scratch=[pltpu.VMEM((rows, BLK), F32)],
        flops=10**8,
        moved=big,
        limit=SMALL,
    )
    got, inner = lax.optimization_barrier((got, inner))
    image_local, coupling = apply_operator(
        stiffness, columns, local, inner, outer, restrict_weights
    )
    weights_out = ((rows, gathered * NB), BF16, "whole")
    cells_all = CROWS * BLK
    part, wh, wl = staged(
        coarse_body,
        [(coarse_rows, "hbm"), (got, "vmem")],
        [part_out, weights_out, weights_out],
        scratch=[
            pltpu.VMEM((CROWS + 1, rows, BLK), F32),
            pltpu.VMEM((rows, cells_all), BF16),
            pltpu.VMEM((rows, cells_all), BF16),
            pltpu.VMEM((cells_all, gathered * NB), BF16),
            pltpu.SemaphoreType.DMA(()),
        ],
        flops=10**9,
        moved=big,
        limit=SMALL,
    )
    got = lax.all_to_all(part, SCATTER, 0, 0, tiled=True)

    msg, u0 = staged(
        first_body,
        [(got, "any"), weights, (start_rows, "whole"), (local_dot, "whole"), (local, "field"),
         (image_local, "field"), (coupling, "field")],
        [msg_out(2), short_out],
        flops=10**8,
        moved=big,
    )
    packet = ((BLK, BLK), F32, "vmem")
    image0, local_image, inner, outer = staged(
        image_body,
        [send, (u0, "whole"), (image_local, "field"), (coupling, "field"), (inv_diag, "field")],
        [field_out, field_out, packet, packet],
        flops=2 * 10**8,
        moved=big,
    )
    inner = lax.ppermute(inner, RING, swaps[0])
    outer = lax.ppermute(outer, RING, swaps[1])
    (image_image,) = apply_operator(stiffness, columns, local_image, inner, outer)

    def exchange(got):
        (part,) = staged(
            apply_body,
            [(wh, "whole"), (wl, "whole"), (got, "vmem")],
            [part_out],
            flops=10**8,
            moved=big,
            limit=SMALL,
        )
        return lax.all_to_all(part, SCATTER, 0, 0, tiled=True)

    got = exchange(lax.all_to_all(msg, GATHER, 0, 0, tiled=True))
    msg, v0 = staged(
        second_body,
        [(got, "any"), (u0, "whole"), weights, (loads, "field"), (image0, "field"),
         (local, "field"), (local_image, "field"), (image_image, "field"),
         (coupling, "field")],
        [msg_out(3), short_out],
        flops=10**8,
        moved=big,
    )
    image1, local_image1 = staged(
        product_body,
        [(v0, "whole"), (image0, "field"), (image_image, "field"), (coupling, "field"),
         (inv_diag, "field")],
        [field_out] * 2,
        flops=2 * 10**8,
        moved=big,
    )
    got = lax.all_to_all(msg, GATHER, 0, 0, tiled=True)
    got, local_image1 = lax.optimization_barrier((got, local_image1))
    got = exchange(got)
    return tuple(
        staged(
            last_body,
            [(got, "any"), (u0, "whole"), (v0, "whole"), weights, (loads, "field"),
             (image0, "field"), (local, "field"), (local_image, "field"), (image1, "field"),
             (local_image1, "field")],
            [field_out] * 3,
            flops=10**8,
            moved=big,
        )
    )


def solution(mesh):
    chips = mesh.devices.reshape(4, 8, 2, mesh.shape["crs"])
    fine = Mesh(chips, RING)
    placed = P(RING)
    return jax.shard_map(
        on_device,
        mesh=fine,
        in_specs=(placed,) * 7 + (P(),),
        out_specs=(placed,) * 3,
        check_vma=False,
    )
```

```python
import functools

import jax
import jax.numpy as jnp
from jax import lax
from jax.experimental import pallas as pl
from jax.experimental.pallas import tpu as pltpu
from jax.sharding import Mesh, PartitionSpec as P

OMEGA = 0.8
SWEEPS = 4
NB = 16
BLK = 128
KB = 6
EXT = 18
DOTS = EXT
ROWS = 24
CROWS = 16
RING = ("y", "z", "core", "crs")
GATHER = ("y", "z")
SCATTER = ("core", "crs")
F32 = jnp.float32
BF16 = jnp.bfloat16
BIG = 60 * 1024 * 1024
SMALL = 12 * 1024 * 1024
TROWS = 24
GROUP = 4
CHUNK = 8


def sweep_coefficients():
    total = [0.0] * SWEEPS
    power = [1.0]
    for _ in range(SWEEPS):
        for i, c in enumerate(power):
            total[i] += c
        grown = [0.0] * (len(power) + 1)
        for i, c in enumerate(power):
            grown[i] += c * (1.0 - OMEGA)
            grown[i + 1] += c * OMEGA
        power = grown
    return total


def split(x):
    high = x.astype(BF16)
    return high, (x - high.astype(F32)).astype(BF16)


def dot(a, b):
    return jnp.dot(a, b, preferred_element_type=F32)


def dot3(a, b):
    ah, al = split(a)
    bh, bl = split(b)
    return dot(ah, bh) + (dot(ah, bl) + dot(al, bh))


def staged(body, ins, outs, scratch=(), flops=0, moved=0, limit=BIG):
    kinds_in = [k for _, k in ins]
    kinds_out = [k for _, _, k in outs]
    n_in, n_out = len(ins), len(outs)
    parts = NB // CHUNK

    def buffer(shape, dtype, kind):
        return pltpu.SMEM(shape, dtype) if kind == "scalar" else pltpu.VMEM(shape, dtype)

    buffers = [buffer(a.shape, a.dtype, k) for a, k in ins if k not in ("vmem", "hbm")]
    buffers += [buffer(sh, dt, k) for sh, dt, k in outs if k != "vmem"]

    def kernel(*refs):
        sources, targets = refs[:n_in], refs[n_in : n_in + n_out]
        rest = list(refs[n_in + n_out :])
        sem_in, sem_out = rest.pop(), rest.pop()
        bufs_in = [r if k in ("vmem", "hbm") else rest.pop(0) for r, k in zip(sources, kinds_in)]
        bufs_out = [r if k == "vmem" else rest.pop(0) for r, k in zip(targets, kinds_out)]

        def chunk(ref, c):
            return ref.at[pl.ds(c * CHUNK, CHUNK)]

        first = [
            pltpu.make_async_copy(s, b, sem_in.at[j, 0])
            for j, (s, b, k) in enumerate(zip(sources, bufs_in, kinds_in))
            if k in ("whole", "scalar", "any")
        ]
        fields = [
            [
                pltpu.make_async_copy(chunk(s, c), chunk(b, c), sem_in.at[j, c])
                for j, (s, b, k) in enumerate(zip(sources, bufs_in, kinds_in))
                if k == "field"
            ]
            for c in range(parts)
        ]
        for copy in first + sum(fields, []):
            copy.start()
        sent = []

        def ready(c):
            for copy in fields[c]:
                copy.wait()

        def emit(n, c=0):
            if kinds_out[n] == "field":
                copy = pltpu.make_async_copy(chunk(bufs_out[n], c), chunk(targets[n], c), sem_out.at[n, c])
            else:
                copy = pltpu.make_async_copy(bufs_out[n], targets[n], sem_out.at[n, 0])
            copy.start()
            sent.append(copy)

        for copy in first:
            copy.wait()
        body(ready, emit, *bufs_in, *bufs_out, *rest)
        for copy in sent:
            copy.wait()

    def spec(kind):
        return pl.BlockSpec(memory_space={"vmem": pltpu.VMEM, "any": pl.ANY}.get(kind, pltpu.HBM))

    return pl.pallas_call(
        kernel,
        out_shape=[jax.ShapeDtypeStruct(sh, dt) for sh, dt, _ in outs],
        in_specs=[spec(k) for k in kinds_in],
        out_specs=[spec(k) for k in kinds_out],
        scratch_shapes=buffers
        + list(scratch)
        + [pltpu.SemaphoreType.DMA((n_out, parts)), pltpu.SemaphoreType.DMA((n_in, parts))],
        compiler_params=pltpu.CompilerParams(vmem_limit_bytes=limit),
        cost_estimate=pl.CostEstimate(flops=flops, bytes_accessed=moved, transcendentals=0),
    )(*[a for a, _ in ins])


def cell_row(map_ref, lane):
    cells = jnp.zeros(lane.shape, jnp.int32)
    for i in range(NB):
        cells = jnp.where(lane % NB == i, map_ref[i], cells)
    return cells


def broadcast(msg_ref, rows):
    for a in range(msg_ref.shape[0]):
        msg_ref[a] = rows


def chunks():
    return [(c, range(c * CHUNK, (c + 1) * CHUNK)) for c in range(NB // CHUNK)]


def start_body(ready, emit, map_ref, w_ref, r_ref, rows_ref):
    wt = w_ref[...].T
    lane = lax.broadcasted_iota(jnp.int32, (1, BLK), 1)
    cells = cell_row(map_ref, lane)
    mine = lane // NB == lax.axis_index(GATHER) % 8
    cells = jnp.where(mine, cells, 0).astype(F32)
    rows = []
    for c, blocks in chunks():
        ready(c)
        rows += [jnp.sum(wt[:, i : i + 1] * r_ref[i], axis=0, keepdims=True) for i in blocks]
    rows_ref[...] = jnp.concatenate(rows + [cells, jnp.zeros((ROWS - NB - 1, BLK), F32)], axis=0)


def group_ghosts(t_ref):
    row = t_ref[0, 1:2]
    for g in range(1, t_ref.shape[0]):
        row = row + t_ref[g, 1:2]
    return row


def open_body(ready, emit, rows_ref, t_ref, msg_ref):
    ghosts = group_ghosts(t_ref)
    lane = lax.broadcasted_iota(jnp.int32, (1, BLK), 1)
    ends = jnp.where(lane < BLK // 2, ghosts[:, :1], ghosts[:, NB - 1 : NB])
    rows = jnp.concatenate([rows_ref[: NB + 1], ends], axis=0)
    broadcast(msg_ref, rows)
    emit(0)


def slot_of(swap):
    return (lax.axis_index("crs") + 1 + swap) % 2


def local_body(ready, emit, send_ref, w_ref, r_ref, d_ref, out_ref, inner_ref, outer_ref, dot_ref):
    total = jnp.zeros((8, BLK), F32)
    for c, blocks in chunks():
        ready(c)
        for i in blocks:
            product = dot3(d_ref[i], r_ref[i])
            out_ref[i] = product
            total = total + fold(r_ref[i] * product)
        emit(0, c)
    dot_ref[...] = total
    emit(3)
    for n, ref in ((0, inner_ref), (1, outer_ref)):
        block = send_ref[0, slot_of(n)]
        ref[:BLK] = out_ref[block]
        ref[BLK:] = jnp.concatenate(
            [w_ref[pl.ds(block, 1), :], jnp.zeros((7, BLK), F32)], axis=0
        )


def target_body(ready, emit, send_ref, map_ref, diag_ref, out_ref):
    slots = 2 * out_ref.shape[0]
    place = lax.axis_index(SCATTER)
    lane = lax.broadcasted_iota(jnp.int32, (1, BLK), 1)
    ghosts = jnp.where(lane == (2 * place + 2) % slots, map_ref[send_ref[0, 1]], 0)
    ghosts = jnp.where(lane == (2 * place + slots - 1) % slots, map_ref[send_ref[0, 0]], ghosts)
    cells = [cell_row(map_ref, lane), ghosts, jnp.zeros((6, BLK), jnp.int32)]
    block = jnp.concatenate([jnp.concatenate(cells, axis=0).astype(F32), diag_ref[...]], axis=0)
    for a in range(out_ref.shape[0]):
        out_ref[a] = block
    emit(0)


def image_body(
    ready, emit, send_ref, u_ref, adr_ref, q_ref, d_ref, im_ref, out_ref, inner_ref, outer_ref
):
    packed = pack(u_ref[...])
    for c, blocks in chunks():
        ready(c)
        for i in blocks:
            image = adr_ref[i] + dot(q_ref[i], packed)
            im_ref[i] = image
            out_ref[i] = dot3(d_ref[i], image)
        emit(0, c)
        emit(1, c)
    for n, ref in ((0, inner_ref), (1, outer_ref)):
        ref[...] = out_ref[send_ref[0, slot_of(n)]]


def product_body(ready, emit, v_ref, im_ref, adim_ref, q_ref, d_ref, az_ref, daz_ref):
    v = v_ref[...]
    alpha = v[EXT : EXT + 1] / v[EXT + 1 : EXT + 2]
    packed = pack(v)
    for c, blocks in chunks():
        ready(c)
        for i in blocks:
            az = im_ref[i] - alpha * (adim_ref[i] + dot(q_ref[i], packed))
            az_ref[i] = az
            daz_ref[i] = dot3(d_ref[i], az)
        emit(0, c)
        emit(1, c)


def solve_rows(cell, inv, use):
    coef = sweep_coefficients()
    lane = lax.broadcasted_iota(jnp.int32, (8, BLK), 1)
    spot = [jnp.where(cell == (lane + BLK * r).astype(F32), 1.0, 0.0) for r in range(CROWS)]
    t = [coef[-1] * spot[r] for r in range(CROWS)]
    for power in range(SWEEPS - 2, -1, -1):
        y = [t[r] * inv[r : r + 1] for r in range(CROWS)]
        new = []
        for r in range(CROWS):
            v = jnp.where(lane == 0, 0.0, pltpu.roll(y[r], 1, 1))
            v = v + jnp.where(lane == BLK - 1, 0.0, pltpu.roll(y[r], BLK - 1, 1))
            if r > 0:
                v = v + y[r - 1]
            if r < CROWS - 1:
                v = v + y[r + 1]
            new.append(v + coef[power] * spot[r])
        t = new
    for r in range(CROWS):
        use(r, t[r] * (inv[r : r + 1] * OMEGA))


def sweep_body(ready, emit, t_ref, out_ref, inv_ref, cell_ref, rows_ref):
    inv = 1.0 / (4.0 + t_ref[0, 8:, :])
    inv_ref[...] = inv
    emit(1)
    devs = t_ref.shape[0]
    own = jnp.concatenate([t_ref[g, :1] for g in range(devs)], axis=0).T
    for g in range(devs):
        cell_ref[g * NB : (g + 1) * NB] = jnp.broadcast_to(own[:NB, g : g + 1], (NB, BLK))
    slots = 2 * devs
    ghosts = jnp.broadcast_to(group_ghosts(t_ref), (8, BLK)).T[:slots, :1]
    row = lax.broadcasted_iota(jnp.int32, (slots, BLK), 0)
    inner = (row > 0) & (row < slots - 1)
    cell_ref[devs * NB :] = jnp.where(inner, ghosts, -1.0)

    def chunk(c, _):
        here = pl.ds(pl.multiple_of(c * 8, 8), 8)

        def use(r, value):
            rows_ref[r, here, :] = value

        solve_rows(cell_ref[here, :], inv, use)
        return 0

    size = cell_ref.shape[0]
    lax.fori_loop(0, size // 8, chunk, 0, unroll=3)
    for r in range(CROWS):
        here = slice(r * BLK, (r + 1) * BLK)
        out_ref[:size, here], out_ref[size:, here] = split(rows_ref[r])
    emit(0)


def spread(part, sums, part_ref):
    devs = part_ref.shape[0]
    part_ref[:, :NB, :] = part[: devs * NB].reshape(devs, NB, BLK)
    for g in range(devs):
        ghosts = part[devs * NB + 2 * g : devs * NB + 2 * g + 2]
        part_ref[g, NB:, :] = jnp.concatenate([ghosts, sums], axis=0)


def coarse_body(
    ready, emit, rows_hbm, inv_hbm, g_ref, part_ref, wh_ref, wl_ref, s_ref, inv_ref, oh_ref, sem
):
    copies = [
        pltpu.make_async_copy(inv_hbm, inv_ref, sem.at[0]),
        pltpu.make_async_copy(rows_hbm, s_ref, sem.at[1]),
    ]
    for copy in copies:
        copy.start()
    devs = g_ref.shape[0]
    sources = devs * NB
    cells = g_ref[:, NB : NB + 1, :].reshape(devs, BLK)
    cells = jnp.sum(cells.reshape(devs // 8, 8, BLK), axis=1)
    sub = lax.broadcasted_iota(jnp.int32, (BLK, BLK), 0)
    for r in range(CROWS):
        index = (sub + r * BLK).astype(F32)
        for q in range(devs // 8):
            hit = jnp.where(cells[q : q + 1] == index, 1.0, 0.0)
            oh_ref[r * BLK : (r + 1) * BLK, q * BLK : (q + 1) * BLK] = hit.astype(BF16)
    place = lax.axis_index(GATHER)
    before = g_ref[(place + devs - 1) % devs][NB + 1 : NB + 2, :1]
    after = g_ref[(place + 1) % devs][NB + 1 : NB + 2, BLK - 1 :]
    row = lax.broadcasted_iota(jnp.int32, (8, BLK), 0)
    outer = jnp.where(row == 0, before, jnp.where(row == 7, after, -1.0))
    for copy in copies:
        copy.wait()
    size = s_ref.shape[0] // 2

    def use(r, value):
        ends = jnp.concatenate([jnp.where(row == 0, value, 0.0), jnp.where(row == 7, value, 0.0)], axis=0)
        here = slice(r * BLK, (r + 1) * BLK)
        for start, piece in zip((size - NB, 2 * size - NB), split(ends)):
            s_ref[start : start + NB, here] += piece

    solve_rows(outer, inv_ref[...], use)
    w = dot(s_ref[...], oh_ref[...])
    w = w[:size] + w[size:]
    wh, wl = split(w)
    wh_ref[...] = wh
    wl_ref[...] = wl
    emit(1)
    emit(2)
    gh, gl = split(g_ref[:, :NB, :].reshape(sources, BLK))
    part = dot(wh, gh) + (dot(wh, gl) + dot(wl, gh))
    spread(part, jnp.zeros((ROWS - EXT, BLK), F32), part_ref)
    emit(0)


def apply_body(ready, emit, wh_ref, wl_ref, g_ref, part_ref):
    devs = g_ref.shape[0]
    gh, gl = split(g_ref[:, :NB, :].reshape(devs * NB, BLK))
    wh = wh_ref[...]
    part = dot(wh, gh) + (dot(wh, gl) + dot(wl_ref[...], gh))
    sums = jnp.sum(g_ref[:, NB:, :], axis=0)
    pad = jnp.zeros((ROWS - DOTS - sums.shape[0], BLK), F32)
    spread(part, jnp.concatenate([sums, pad], axis=0), part_ref)
    emit(0)


def operator_kernel(first, cols_hbm, s_hbm, f_hbm, inner_hbm, outer_hbm, *rest):
    if first:
        (w_hbm, out_hbm, q_hbm, cols_ref, s_ref, f_ref, inner_ref, outer_ref, out_ref, xh, sem, out_sem,
         w_ref, q_ref, xl) = rest
    else:
        out_hbm, cols_ref, s_ref, f_ref, inner_ref, outer_ref, out_ref, xh, sem, out_sem = rest
    steps = NB // GROUP

    def part(ref, g):
        return ref.at[pl.ds(g * GROUP, GROUP)]

    def block(g):
        return pltpu.make_async_copy(part(s_hbm, g), part(s_ref, g), sem.at[g])

    def result(n, g):
        source, target = ((out_ref, out_hbm), (q_ref, q_hbm))[n] if first else (out_ref, out_hbm)
        return pltpu.make_async_copy(part(source, g), part(target, g), out_sem.at[n, g])

    pairs = [(cols_hbm, cols_ref), (f_hbm, f_ref), (inner_hbm, inner_ref), (outer_hbm, outer_ref)]
    if first:
        pairs.append((w_hbm, w_ref))
    head = [pltpu.make_async_copy(a, b, sem.at[steps + n]) for n, (a, b) in enumerate(pairs)]
    for copy in head:
        copy.start()
    for g in range(steps):
        block(g).start()
    for copy in head:
        copy.wait()
    lane = lax.broadcasted_iota(jnp.int32, (BLK, BLK), 1)
    odd = lax.axis_index("crs") % 2 == 1

    def lower(rows):
        return jnp.where(odd, inner_ref[rows, :], outer_ref[rows, :])

    def upper(rows):
        return jnp.where(odd, outer_ref[rows, :], inner_ref[rows, :])

    if first:
        wt = w_ref[...].T
        turned = jnp.concatenate([lower(slice(BLK, None)), upper(slice(BLK, None))], axis=0).T
    for e in range(EXT):
        x = f_ref[e] if e < NB else (lower, upper)[e - NB](slice(0, BLK))
        high, low = split(x)
        xh[e, :, :BLK] = high
        if first:
            xl[e, :, :BLK] = low
            at = 8 * (e - NB)
            col = wt[:, e : e + 1] if e < NB else turned[:, at : at + 1]
            high, low = split(jnp.where((lane % 32 == e) & (lane < 96), col, 0.0))
            xh[e, :, BLK:] = high
            xl[e, :, BLK:] = low
        else:
            xh[e, :, BLK:] = low

    def step(g, _):
        block(g).wait()
        for b in range(GROUP):
            i = g * GROUP + b
            sh, sl, vh, vl = [], [], [], []
            for k in range(KB):
                col = cols_ref[k, i]
                high, low = split(s_ref[i, k])
                sh.append(high)
                sl.append(low)
                vh.append(xh[col])
                if first:
                    vl.append(xl[col])
            sh = jnp.concatenate(sh, axis=1)
            both = jnp.concatenate([sh, jnp.concatenate(sl, axis=1)], axis=0)
            image = dot(both, jnp.concatenate(vh, axis=0))
            if first:
                image = image[:BLK] + (image[BLK:] + dot(sh, jnp.concatenate(vl, axis=0)))
                high, low = split(image[:, BLK:])
                q_ref[i] = jnp.where((lane >= 32) & (lane < 64), low.astype(F32), high.astype(F32)).astype(BF16)
                image = image[:, :BLK]
            else:
                image = image[:BLK, :BLK] + (image[:BLK, BLK:] + image[BLK:, :BLK])
            out_ref[i] = image
        result(0, g).start()
        if first:
            result(1, g).start()
        return 0

    lax.fori_loop(0, steps, step, 0)
    for g in range(steps):
        result(0, g).wait()
        if first:
            result(1, g).wait()


def pack(u):
    keep = lax.broadcasted_iota(jnp.int32, (ROWS, BLK), 0) < EXT
    u = jnp.concatenate([jnp.where(keep, u, 0.0), jnp.zeros((32 - ROWS, BLK), F32)], axis=0)
    high, low = split(u)
    return jnp.concatenate([high, high, low, jnp.zeros((32, BLK), BF16)], axis=0)


def fold_rows(x):
    return jnp.sum(x.reshape(NB // 8, 8, BLK), axis=0)


def fold(x):
    return jnp.sum(x.reshape(BLK // 8, 8, BLK), axis=0)


def message(rows, dots):
    sums = [jnp.sum(d, axis=0, keepdims=True) for d in dots]
    return jnp.concatenate(rows + sums, axis=0)


def first_body(
    ready, emit, got_ref, w_ref, rows_ref, dot_ref, dr_ref, adr_ref, q_ref, msg_ref, u_ref
):
    u = jnp.sum(got_ref[...], axis=0)
    u_ref[...] = u
    emit(1)
    packed = pack(u)
    wt = w_ref[...].T
    rows = []
    rz = dot_ref[...] + fold_rows(rows_ref[:NB] * u[:NB])
    zw = jnp.zeros((8, BLK), F32)
    for c, blocks in chunks():
        ready(c)
        for i in blocks:
            col = wt[:, i : i + 1]
            image = adr_ref[i] + dot(q_ref[i], packed)
            rows.append(jnp.sum(col * image, axis=0, keepdims=True))
            zw = zw + fold((dr_ref[i] + col * u[i : i + 1]) * image)
    broadcast(msg_ref, message(rows, [rz, zw]))
    emit(0)


def second_body(
    ready, emit, got_ref, u_ref, w_ref, r_ref, im_ref, dr_ref, dim_ref, adim_ref, q_ref,
    msg_ref, v_ref,
):
    v = jnp.sum(got_ref[...], axis=0)
    v_ref[...] = v
    emit(1)
    alpha = v[EXT : EXT + 1] / v[EXT + 1 : EXT + 2]
    u0 = u_ref[...]
    u1 = u0 - alpha * v
    packed = pack(v)
    wt = w_ref[...].T
    rows = []
    rz = jnp.zeros((8, BLK), F32)
    zaz = jnp.zeros((8, BLK), F32)
    cross = jnp.zeros((8, BLK), F32)
    for c, blocks in chunks():
        ready(c)
        for i in blocks:
            col = wt[:, i : i + 1]
            image = im_ref[i]
            dr = dr_ref[i]
            z0 = dr + col * u0[i : i + 1]
            z1 = dr - alpha * dim_ref[i] + col * u1[i : i + 1]
            az = image - alpha * (adim_ref[i] + dot(q_ref[i], packed))
            rows.append(jnp.sum(col * az, axis=0, keepdims=True))
            rz = rz + fold((r_ref[i] - alpha * image) * z1)
            zaz = zaz + fold(z1 * az)
            cross = cross + fold(z1 * image + z0 * az)
    broadcast(msg_ref, message(rows, [rz, zaz, cross]))
    emit(0)


def last_body(
    ready, emit, got_ref, u_ref, v_ref, w_ref, r_ref, im_ref, dr_ref, dim_ref, az_ref, daz_ref,
    sol_ref, res_ref, pre_ref,
):
    t = jnp.sum(got_ref[...], axis=0)
    v = v_ref[...]
    gamma0 = v[EXT : EXT + 1]
    curve0 = v[EXT + 1 : EXT + 2]
    gamma1 = t[EXT : EXT + 1]
    alpha0 = gamma0 / curve0
    beta = gamma1 / gamma0
    curve1 = t[EXT + 1 : EXT + 2] + beta * (t[EXT + 2 : EXT + 3] + beta * curve0)
    alpha1 = gamma1 / curve1
    u0 = u_ref[...]
    u1 = u0 - alpha0 * v
    u2 = u1 - alpha1 * (t + beta * v)
    wt = w_ref[...].T
    for c, blocks in chunks():
        ready(c)
        for i in blocks:
            col = wt[:, i : i + 1]
            image = im_ref[i]
            dr = dr_ref[i]
            dim = dim_ref[i]
            z0 = dr + col * u0[i : i + 1]
            dr1 = dr - alpha0 * dim
            z1 = dr1 + col * u1[i : i + 1]
            sol_ref[i] = alpha0 * z0 + alpha1 * (z1 + beta * z0)
            res_ref[i] = r_ref[i] - alpha0 * image - alpha1 * (az_ref[i] + beta * image)
            local = dr1 - alpha1 * (daz_ref[i] + beta * dim)
            pre_ref[i] = local + col * u2[i : i + 1]
        for n in range(3):
            emit(n, c)


FIELD = (NB, BLK, BLK)


def apply_operator(stiffness, columns, field, inner, outer, weights=None):
    first = weights is not None
    hbm = pl.BlockSpec(memory_space=pltpu.HBM)
    outs = [jax.ShapeDtypeStruct(FIELD, F32)]
    args = [columns, stiffness, field, inner, outer]
    scratch = [
        pltpu.SMEM(columns.shape, jnp.int32),
        pltpu.VMEM(stiffness.shape, F32),
        pltpu.VMEM(FIELD, F32),
        pltpu.VMEM(inner.shape, F32),
        pltpu.VMEM(outer.shape, F32),
        pltpu.VMEM(FIELD, F32),
        pltpu.VMEM((EXT, BLK, 2 * BLK), BF16),
        pltpu.SemaphoreType.DMA((NB // GROUP + 5,)),
        pltpu.SemaphoreType.DMA((2, NB // GROUP)),
    ]
    if first:
        outs.append(jax.ShapeDtypeStruct(FIELD, BF16))
        args.append(weights)
        scratch += [
            pltpu.VMEM(weights.shape, F32),
            pltpu.VMEM(FIELD, BF16),
            pltpu.VMEM((EXT, BLK, 2 * BLK), BF16),
        ]
    return pl.pallas_call(
        functools.partial(operator_kernel, first),
        out_shape=outs,
        in_specs=[hbm] * 3 + [pl.BlockSpec(memory_space=pl.ANY)] * 2 + [hbm] * (len(args) - 5),
        out_specs=[hbm] * len(outs),
        scratch_shapes=scratch,
        compiler_params=pltpu.CompilerParams(vmem_limit_bytes=BIG),
        cost_estimate=pl.CostEstimate(flops=6 * 10**9, bytes_accessed=8 << 20, transcendentals=0),
    )(*args)


def on_device(
    loads, stiffness, inv_diag, columns, send_lists, restrict_weights, coarse_map, coarse_diag
):
    devices = lax.axis_size(RING)
    gathered = lax.axis_size(GATHER)
    scattered = lax.axis_size(SCATTER)
    swaps = []
    for first in (0, 1):
        pairs = [((first + 2 * i) % devices, (first + 2 * i + 1) % devices) for i in range(devices // 2)]
        swaps.append(pairs + [(j, i) for i, j in pairs])
    send = (send_lists.reshape(1, 2), "scalar")
    cells = (coarse_map, "scalar")
    columns = columns.T
    weights = (restrict_weights, "whole")

    def msg_out(extra):
        return ((gathered, NB + extra, BLK), F32, "whole")

    part_shape = (scattered, ROWS, BLK)
    part_out = (part_shape, F32, "whole")
    short_out = (part_shape[1:], F32, "whole")
    field_out = (FIELD, F32, "field")
    big = 2 << 20

    (target,) = staged(
        target_body,
        [send, cells, (coarse_diag, "whole")],
        [((scattered, TROWS, BLK), F32, "whole")],
        moved=1 << 18,
    )
    targets = lax.all_to_all(target, SCATTER, 0, 0, tiled=True)
    (start_rows,) = staged(
        start_body,
        [cells, weights, (loads, "field")],
        [((ROWS, BLK), F32, "vmem")],
        flops=10**6,
        moved=big,
    )
    (msg,) = staged(
        open_body, [(start_rows, "vmem"), (targets, "vmem")], [msg_out(2)], moved=1 << 18, limit=SMALL
    )
    got = lax.all_to_all(msg, GATHER, 0, 0, tiled=True)
    packet = ((BLK + 8, BLK), F32, "vmem")
    local, inner, outer, local_dot = staged(
        local_body,
        [send, weights, (loads, "field"), (inv_diag, "field")],
        [field_out, packet, packet, ((8, BLK), F32, "whole")],
        flops=2 * 10**8,
        moved=big,
    )
    inner = lax.ppermute(inner, RING, swaps[0])
    outer = lax.ppermute(outer, RING, swaps[1])
    rows = scattered * EXT
    coarse_rows, coarse_inv = staged(
        sweep_body,
        [(targets, "vmem")],
        [((2 * rows, CROWS * BLK), BF16, "whole"), ((CROWS, BLK), F32, "whole")],
        scratch=[pltpu.VMEM((rows, BLK), F32), pltpu.VMEM((CROWS, rows, BLK), F32)],
        flops=10**8,
        moved=big,
        limit=SMALL,
    )
    got, inner = lax.optimization_barrier((got, inner))
    image_local, coupling = apply_operator(
        stiffness, columns, local, inner, outer, restrict_weights
    )
    weights_out = ((rows, gathered * NB), BF16, "whole")
    cells_all = CROWS * BLK
    part, wh, wl = staged(
        coarse_body,
        [(coarse_rows, "hbm"), (coarse_inv, "hbm"), (got, "vmem")],
        [part_out, weights_out, weights_out],
        scratch=[
            pltpu.VMEM((2 * rows, cells_all), BF16),
            pltpu.VMEM((CROWS, BLK), F32),
            pltpu.VMEM((cells_all, gathered * NB), BF16),
            pltpu.SemaphoreType.DMA((2,)),
        ],
        flops=10**9,
        moved=big,
        limit=SMALL,
    )
    got = lax.all_to_all(part, SCATTER, 0, 0, tiled=True)

    msg, u0 = staged(
        first_body,
        [(got, "any"), weights, (start_rows, "whole"), (local_dot, "whole"), (local, "field"),
         (image_local, "field"), (coupling, "field")],
        [msg_out(2), short_out],
        flops=10**8,
        moved=big,
    )
    packet = ((BLK, BLK), F32, "vmem")
    image0, local_image, inner, outer = staged(
        image_body,
        [send, (u0, "whole"), (image_local, "field"), (coupling, "field"), (inv_diag, "field")],
        [field_out, field_out, packet, packet],
        flops=2 * 10**8,
        moved=big,
    )
    inner = lax.ppermute(inner, RING, swaps[0])
    outer = lax.ppermute(outer, RING, swaps[1])
    (image_image,) = apply_operator(stiffness, columns, local_image, inner, outer)

    def exchange(got):
        (part,) = staged(
            apply_body,
            [(wh, "whole"), (wl, "whole"), (got, "vmem")],
            [part_out],
            flops=10**8,
            moved=big,
            limit=SMALL,
        )
        return lax.all_to_all(part, SCATTER, 0, 0, tiled=True)

    got = exchange(lax.all_to_all(msg, GATHER, 0, 0, tiled=True))
    msg, v0 = staged(
        second_body,
        [(got, "any"), (u0, "whole"), weights, (loads, "field"), (image0, "field"),
         (local, "field"), (local_image, "field"), (image_image, "field"),
         (coupling, "field")],
        [msg_out(3), short_out],
        flops=10**8,
        moved=big,
    )
    image1, local_image1 = staged(
        product_body,
        [(v0, "whole"), (image0, "field"), (image_image, "field"), (coupling, "field"),
         (inv_diag, "field")],
        [field_out] * 2,
        flops=2 * 10**8,
        moved=big,
    )
    got = lax.all_to_all(msg, GATHER, 0, 0, tiled=True)
    got, local_image1 = lax.optimization_barrier((got, local_image1))
    got = exchange(got)
    return tuple(
        staged(
            last_body,
            [(got, "any"), (u0, "whole"), (v0, "whole"), weights, (loads, "field"),
             (image0, "field"), (local, "field"), (local_image, "field"), (image1, "field"),
             (local_image1, "field")],
            [field_out] * 3,
            flops=10**8,
            moved=big,
        )
    )


def solution(mesh):
    chips = mesh.devices.reshape(4, 8, 2, mesh.shape["crs"])
    fine = Mesh(chips, RING)
    placed = P(RING)
    return jax.shard_map(
        on_device,
        mesh=fine,
        in_specs=(placed,) * 7 + (P(),),
        out_specs=(placed,) * 3,
        check_vma=False,
    )
```

```python
import functools

import jax
import jax.numpy as jnp
from jax import lax
from jax.experimental import pallas as pl
from jax.experimental.pallas import tpu as pltpu
from jax.sharding import Mesh, PartitionSpec as P

OMEGA = 0.8
SWEEPS = 4
NB = 16
BLK = 128
KB = 6
EXT = 18
DOTS = EXT
ROWS = 22
CROWS = 16
RING = ("y", "z", "core", "crs")
GATHER = ("y", "z")
SCATTER = ("core", "crs")
F32 = jnp.float32
BF16 = jnp.bfloat16
BIG = 60 * 1024 * 1024
SMALL = 12 * 1024 * 1024
TROWS = 24
GROUP = 4
CHUNK = 8


def sweep_coefficients():
    total = [0.0] * SWEEPS
    power = [1.0]
    for _ in range(SWEEPS):
        for i, c in enumerate(power):
            total[i] += c
        grown = [0.0] * (len(power) + 1)
        for i, c in enumerate(power):
            grown[i] += c * (1.0 - OMEGA)
            grown[i + 1] += c * OMEGA
        power = grown
    return total


def split(x):
    high = x.astype(BF16)
    return high, (x - high.astype(F32)).astype(BF16)


def dot(a, b):
    return jnp.dot(a, b, preferred_element_type=F32)


def dot3(a, b):
    ah, al = split(a)
    bh, bl = split(b)
    return dot(ah, bh) + (dot(ah, bl) + dot(al, bh))


def staged(body, ins, outs, scratch=(), flops=0, moved=0, limit=BIG):
    kinds_in = [k for _, k in ins]
    kinds_out = [k for _, _, k in outs]
    n_in, n_out = len(ins), len(outs)
    parts = NB // CHUNK

    def buffer(shape, dtype, kind):
        return pltpu.SMEM(shape, dtype) if kind == "scalar" else pltpu.VMEM(shape, dtype)

    buffers = [buffer(a.shape, a.dtype, k) for a, k in ins if k not in ("vmem", "hbm")]
    buffers += [buffer(sh, dt, k) for sh, dt, k in outs if k != "vmem"]

    def kernel(*refs):
        sources, targets = refs[:n_in], refs[n_in : n_in + n_out]
        rest = list(refs[n_in + n_out :])
        sem_in, sem_out = rest.pop(), rest.pop()
        bufs_in = [r if k in ("vmem", "hbm") else rest.pop(0) for r, k in zip(sources, kinds_in)]
        bufs_out = [r if k == "vmem" else rest.pop(0) for r, k in zip(targets, kinds_out)]

        def chunk(ref, c):
            return ref.at[pl.ds(c * CHUNK, CHUNK)]

        first = [
            pltpu.make_async_copy(s, b, sem_in.at[j, 0])
            for j, (s, b, k) in enumerate(zip(sources, bufs_in, kinds_in))
            if k in ("whole", "scalar", "any")
        ]
        fields = [
            [
                pltpu.make_async_copy(chunk(s, c), chunk(b, c), sem_in.at[j, c])
                for j, (s, b, k) in enumerate(zip(sources, bufs_in, kinds_in))
                if k == "field"
            ]
            for c in range(parts)
        ]
        for copy in first + sum(fields, []):
            copy.start()
        sent = []

        def ready(c):
            for copy in fields[c]:
                copy.wait()

        def emit(n, c=0):
            if kinds_out[n] == "field":
                copy = pltpu.make_async_copy(chunk(bufs_out[n], c), chunk(targets[n], c), sem_out.at[n, c])
            else:
                copy = pltpu.make_async_copy(bufs_out[n], targets[n], sem_out.at[n, 0])
            copy.start()
            sent.append(copy)

        for copy in first:
            copy.wait()
        body(ready, emit, *bufs_in, *bufs_out, *rest)
        for copy in sent:
            copy.wait()

    def spec(kind):
        return pl.BlockSpec(memory_space={"vmem": pltpu.VMEM, "any": pl.ANY}.get(kind, pltpu.HBM))

    return pl.pallas_call(
        kernel,
        out_shape=[jax.ShapeDtypeStruct(sh, dt) for sh, dt, _ in outs],
        in_specs=[spec(k) for k in kinds_in],
        out_specs=[spec(k) for k in kinds_out],
        scratch_shapes=buffers
        + list(scratch)
        + [pltpu.SemaphoreType.DMA((n_out, parts)), pltpu.SemaphoreType.DMA((n_in, parts))],
        compiler_params=pltpu.CompilerParams(vmem_limit_bytes=limit),
        cost_estimate=pl.CostEstimate(flops=flops, bytes_accessed=moved, transcendentals=0),
    )(*[a for a, _ in ins])


def cell_row(map_ref, lane):
    cells = jnp.zeros(lane.shape, jnp.int32)
    for i in range(NB):
        cells = jnp.where(lane % NB == i, map_ref[i], cells)
    return cells


def broadcast(msg_ref, rows):
    for a in range(msg_ref.shape[0]):
        msg_ref[a] = rows


def chunks():
    return [(c, range(c * CHUNK, (c + 1) * CHUNK)) for c in range(NB // CHUNK)]


def start_body(ready, emit, map_ref, w_ref, r_ref, rows_ref):
    wt = w_ref[...].T
    lane = lax.broadcasted_iota(jnp.int32, (1, BLK), 1)
    cells = cell_row(map_ref, lane)
    mine = lane // NB == lax.axis_index(GATHER) % 8
    cells = jnp.where(mine, cells, 0).astype(F32)
    rows = []
    for c, blocks in chunks():
        ready(c)
        rows += [jnp.sum(wt[:, i : i + 1] * r_ref[i], axis=0, keepdims=True) for i in blocks]
    rows_ref[...] = jnp.concatenate(rows + [cells, jnp.zeros((ROWS - NB - 1, BLK), F32)], axis=0)


def group_ghosts(t_ref):
    row = t_ref[0, 1:2]
    for g in range(1, t_ref.shape[0]):
        row = row + t_ref[g, 1:2]
    return row


def open_body(ready, emit, rows_ref, t_ref, msg_ref):
    ghosts = group_ghosts(t_ref)
    lane = lax.broadcasted_iota(jnp.int32, (1, BLK), 1)
    ends = jnp.where(lane < BLK // 2, ghosts[:, :1], ghosts[:, NB - 1 : NB])
    rows = jnp.concatenate([rows_ref[: NB + 1], ends], axis=0)
    broadcast(msg_ref, rows)
    emit(0)


def slot_of(swap):
    return (lax.axis_index("crs") + 1 + swap) % 2


def local_body(ready, emit, send_ref, w_ref, r_ref, d_ref, out_ref, inner_ref, outer_ref, dot_ref):
    total = jnp.zeros((8, BLK), F32)
    for c, blocks in chunks():
        ready(c)
        for i in blocks:
            product = dot3(d_ref[i], r_ref[i])
            out_ref[i] = product
            total = total + fold(r_ref[i] * product)
        emit(0, c)
    dot_ref[...] = total
    emit(3)
    for n, ref in ((0, inner_ref), (1, outer_ref)):
        block = send_ref[0, slot_of(n)]
        ref[:BLK] = out_ref[block]
        ref[BLK:] = jnp.concatenate(
            [w_ref[pl.ds(block, 1), :], jnp.zeros((7, BLK), F32)], axis=0
        )


def target_body(ready, emit, send_ref, map_ref, diag_ref, out_ref):
    slots = 2 * out_ref.shape[0]
    place = lax.axis_index(SCATTER)
    lane = lax.broadcasted_iota(jnp.int32, (1, BLK), 1)
    ghosts = jnp.where(lane == (2 * place + 2) % slots, map_ref[send_ref[0, 1]], 0)
    ghosts = jnp.where(lane == (2 * place + slots - 1) % slots, map_ref[send_ref[0, 0]], ghosts)
    cells = [cell_row(map_ref, lane), ghosts, jnp.zeros((6, BLK), jnp.int32)]
    block = jnp.concatenate([jnp.concatenate(cells, axis=0).astype(F32), diag_ref[...]], axis=0)
    for a in range(out_ref.shape[0]):
        out_ref[a] = block
    emit(0)


def image_body(
    ready, emit, send_ref, u_ref, adr_ref, q_ref, d_ref, im_ref, out_ref, inner_ref, outer_ref
):
    packed = pack(u_ref[...])
    for c, blocks in chunks():
        ready(c)
        for i in blocks:
            image = adr_ref[i] + dot(q_ref[i], packed)
            im_ref[i] = image
            out_ref[i] = dot3(d_ref[i], image)
        emit(0, c)
        emit(1, c)
    for n, ref in ((0, inner_ref), (1, outer_ref)):
        ref[...] = out_ref[send_ref[0, slot_of(n)]]


def product_body(ready, emit, v_ref, im_ref, adim_ref, q_ref, d_ref, az_ref, daz_ref):
    v = v_ref[...]
    alpha = v[EXT : EXT + 1] / v[EXT + 1 : EXT + 2]
    packed = pack(v)
    for c, blocks in chunks():
        ready(c)
        for i in blocks:
            az = im_ref[i] - alpha * (adim_ref[i] + dot(q_ref[i], packed))
            az_ref[i] = az
            daz_ref[i] = dot3(d_ref[i], az)
        emit(0, c)
        emit(1, c)


def solve_rows(cell, inv, use):
    coef = sweep_coefficients()
    lane = lax.broadcasted_iota(jnp.int32, (8, BLK), 1)
    spot = [jnp.where(cell == (lane + BLK * r).astype(F32), 1.0, 0.0) for r in range(CROWS)]
    t = [coef[-1] * spot[r] for r in range(CROWS)]
    for power in range(SWEEPS - 2, -1, -1):
        y = [t[r] * inv[r : r + 1] for r in range(CROWS)]
        new = []
        for r in range(CROWS):
            v = jnp.where(lane == 0, 0.0, pltpu.roll(y[r], 1, 1))
            v = v + jnp.where(lane == BLK - 1, 0.0, pltpu.roll(y[r], BLK - 1, 1))
            if r > 0:
                v = v + y[r - 1]
            if r < CROWS - 1:
                v = v + y[r + 1]
            new.append(v + coef[power] * spot[r])
        t = new
    for r in range(CROWS):
        use(r, t[r] * (inv[r : r + 1] * OMEGA))


def sweep_body(ready, emit, t_ref, out_ref, inv_ref, cell_ref, rows_ref):
    inv = 1.0 / (4.0 + t_ref[0, 8:, :])
    inv_ref[...] = inv
    emit(1)
    devs = t_ref.shape[0]
    own = jnp.concatenate([t_ref[g, :1] for g in range(devs)], axis=0).T
    for g in range(devs):
        cell_ref[g * NB : (g + 1) * NB] = jnp.broadcast_to(own[:NB, g : g + 1], (NB, BLK))
    slots = 2 * devs
    ghosts = jnp.broadcast_to(group_ghosts(t_ref), (8, BLK)).T[:slots, :1]
    row = lax.broadcasted_iota(jnp.int32, (slots, BLK), 0)
    inner = (row > 0) & (row < slots - 1)
    cell_ref[devs * NB :] = jnp.where(inner, ghosts, -1.0)

    def chunk(c, _):
        here = pl.ds(pl.multiple_of(c * 8, 8), 8)

        def use(r, value):
            rows_ref[r, here, :] = value

        solve_rows(cell_ref[here, :], inv, use)
        return 0

    size = cell_ref.shape[0]
    lax.fori_loop(0, size // 8, chunk, 0, unroll=3)
    for r in range(CROWS):
        here = slice(r * BLK, (r + 1) * BLK)
        out_ref[:size, here], out_ref[size:, here] = split(rows_ref[r])
    emit(0)


def spread(part, sums, part_ref):
    devs = part_ref.shape[0]
    part_ref[:, :NB, :] = part[: devs * NB].reshape(devs, NB, BLK)
    for g in range(devs):
        ghosts = part[devs * NB + 2 * g : devs * NB + 2 * g + 2]
        part_ref[g, NB:, :] = jnp.concatenate([ghosts, sums], axis=0)


def coarse_body(
    ready, emit, rows_hbm, inv_hbm, g_ref, part_ref, wh_ref, wl_ref, s_ref, inv_ref, oh_ref, sem
):
    copies = [
        pltpu.make_async_copy(inv_hbm, inv_ref, sem.at[0]),
        pltpu.make_async_copy(rows_hbm, s_ref, sem.at[1]),
    ]
    for copy in copies:
        copy.start()
    devs = g_ref.shape[0]
    sources = devs * NB
    cells = g_ref[:, NB : NB + 1, :].reshape(devs, BLK)
    cells = jnp.sum(cells.reshape(devs // 8, 8, BLK), axis=1)
    sub = lax.broadcasted_iota(jnp.int32, (BLK, BLK), 0)
    for r in range(CROWS):
        index = (sub + r * BLK).astype(F32)
        for q in range(devs // 8):
            hit = jnp.where(cells[q : q + 1] == index, 1.0, 0.0)
            oh_ref[r * BLK : (r + 1) * BLK, q * BLK : (q + 1) * BLK] = hit.astype(BF16)
    place = lax.axis_index(GATHER)
    before = g_ref[(place + devs - 1) % devs][NB + 1 : NB + 2, :1]
    after = g_ref[(place + 1) % devs][NB + 1 : NB + 2, BLK - 1 :]
    row = lax.broadcasted_iota(jnp.int32, (8, BLK), 0)
    outer = jnp.where(row == 0, before, jnp.where(row == 7, after, -1.0))
    for copy in copies:
        copy.wait()
    size = s_ref.shape[0] // 2

    def use(r, value):
        ends = jnp.concatenate([jnp.where(row == 0, value, 0.0), jnp.where(row == 7, value, 0.0)], axis=0)
        here = slice(r * BLK, (r + 1) * BLK)
        for start, piece in zip((size - NB, 2 * size - NB), split(ends)):
            s_ref[start : start + NB, here] += piece

    solve_rows(outer, inv_ref[...], use)
    w = dot(s_ref[...], oh_ref[...])
    w = w[:size] + w[size:]
    wh, wl = split(w)
    wh_ref[...] = wh
    wl_ref[...] = wl
    emit(1)
    emit(2)
    gh, gl = split(g_ref[:, :NB, :].reshape(sources, BLK))
    part = dot(wh, gh) + (dot(wh, gl) + dot(wl, gh))
    spread(part, jnp.zeros((ROWS - EXT, BLK), F32), part_ref)
    emit(0)


def apply_body(ready, emit, wh_ref, wl_ref, g_ref, part_ref):
    devs = g_ref.shape[0]
    gh, gl = split(g_ref[:, :NB, :].reshape(devs * NB, BLK))
    wh = wh_ref[...]
    part = dot(wh, gh) + (dot(wh, gl) + dot(wl_ref[...], gh))
    sums = jnp.sum(g_ref[:, NB:, :], axis=0)
    pad = jnp.zeros((ROWS - DOTS - sums.shape[0], BLK), F32)
    spread(part, jnp.concatenate([sums, pad], axis=0), part_ref)
    emit(0)


def operator_kernel(first, cols_hbm, s_hbm, f_hbm, inner_hbm, outer_hbm, *rest):
    if first:
        (w_hbm, out_hbm, q_hbm, cols_ref, s_ref, f_ref, inner_ref, outer_ref, out_ref, xh, sem, out_sem,
         w_ref, q_ref, xl) = rest
    else:
        out_hbm, cols_ref, s_ref, f_ref, inner_ref, outer_ref, out_ref, xh, sem, out_sem = rest
    steps = NB // GROUP

    def part(ref, g):
        return ref.at[pl.ds(g * GROUP, GROUP)]

    def block(g):
        return pltpu.make_async_copy(part(s_hbm, g), part(s_ref, g), sem.at[g])

    def result(n, g):
        source, target = ((out_ref, out_hbm), (q_ref, q_hbm))[n] if first else (out_ref, out_hbm)
        return pltpu.make_async_copy(part(source, g), part(target, g), out_sem.at[n, g])

    pairs = [(cols_hbm, cols_ref), (f_hbm, f_ref), (inner_hbm, inner_ref), (outer_hbm, outer_ref)]
    if first:
        pairs.append((w_hbm, w_ref))
    head = [pltpu.make_async_copy(a, b, sem.at[steps + n]) for n, (a, b) in enumerate(pairs)]
    for copy in head:
        copy.start()
    for g in range(steps):
        block(g).start()
    for copy in head:
        copy.wait()
    lane = lax.broadcasted_iota(jnp.int32, (BLK, BLK), 1)
    odd = lax.axis_index("crs") % 2 == 1

    def lower(rows):
        return jnp.where(odd, inner_ref[rows, :], outer_ref[rows, :])

    def upper(rows):
        return jnp.where(odd, outer_ref[rows, :], inner_ref[rows, :])

    if first:
        wt = w_ref[...].T
        turned = jnp.concatenate([lower(slice(BLK, None)), upper(slice(BLK, None))], axis=0).T
    for e in range(EXT):
        x = f_ref[e] if e < NB else (lower, upper)[e - NB](slice(0, BLK))
        high, low = split(x)
        xh[e, :, :BLK] = high
        if first:
            xl[e, :, :BLK] = low
            at = 8 * (e - NB)
            col = wt[:, e : e + 1] if e < NB else turned[:, at : at + 1]
            high, low = split(jnp.where((lane % 32 == e) & (lane < 96), col, 0.0))
            xh[e, :, BLK:] = high
            xl[e, :, BLK:] = low
        else:
            xh[e, :, BLK:] = low

    def step(g, _):
        block(g).wait()
        for b in range(GROUP):
            i = g * GROUP + b
            sh, sl, vh, vl = [], [], [], []
            for k in range(KB):
                col = cols_ref[k, i]
                high, low = split(s_ref[i, k])
                sh.append(high)
                sl.append(low)
                vh.append(xh[col])
                if first:
                    vl.append(xl[col])
            sh = jnp.concatenate(sh, axis=1)
            both = jnp.concatenate([sh, jnp.concatenate(sl, axis=1)], axis=0)
            image = dot(both, jnp.concatenate(vh, axis=0))
            if first:
                image = image[:BLK] + (image[BLK:] + dot(sh, jnp.concatenate(vl, axis=0)))
                high, low = split(image[:, BLK:])
                q_ref[i] = jnp.where((lane >= 32) & (lane < 64), low.astype(F32), high.astype(F32)).astype(BF16)
                image = image[:, :BLK]
            else:
                image = image[:BLK, :BLK] + (image[:BLK, BLK:] + image[BLK:, :BLK])
            out_ref[i] = image
        result(0, g).start()
        if first:
            result(1, g).start()
        return 0

    lax.fori_loop(0, steps, step, 0)
    for g in range(steps):
        result(0, g).wait()
        if first:
            result(1, g).wait()


def pack(u):
    keep = lax.broadcasted_iota(jnp.int32, (ROWS, BLK), 0) < EXT
    u = jnp.concatenate([jnp.where(keep, u, 0.0), jnp.zeros((32 - ROWS, BLK), F32)], axis=0)
    high, low = split(u)
    return jnp.concatenate([high, high, low, jnp.zeros((32, BLK), BF16)], axis=0)


def fold_rows(x):
    return jnp.sum(x.reshape(NB // 8, 8, BLK), axis=0)


def fold(x):
    return jnp.sum(x.reshape(BLK // 8, 8, BLK), axis=0)


def message(rows, dots):
    sums = [jnp.sum(d, axis=0, keepdims=True) for d in dots]
    return jnp.concatenate(rows + sums, axis=0)


def first_body(
    ready, emit, got_ref, w_ref, rows_ref, dot_ref, dr_ref, adr_ref, q_ref, msg_ref, u_ref
):
    u = jnp.sum(got_ref[...], axis=0)
    u_ref[...] = u
    emit(1)
    packed = pack(u)
    wt = w_ref[...].T
    rows = []
    rz = dot_ref[...] + fold_rows(rows_ref[:NB] * u[:NB])
    zw = jnp.zeros((8, BLK), F32)
    for c, blocks in chunks():
        ready(c)
        for i in blocks:
            col = wt[:, i : i + 1]
            image = adr_ref[i] + dot(q_ref[i], packed)
            rows.append(jnp.sum(col * image, axis=0, keepdims=True))
            zw = zw + fold((dr_ref[i] + col * u[i : i + 1]) * image)
    broadcast(msg_ref, message(rows, [rz, zw]))
    emit(0)


def second_body(
    ready, emit, got_ref, u_ref, w_ref, r_ref, im_ref, dr_ref, dim_ref, adim_ref, q_ref,
    msg_ref, v_ref,
):
    v = jnp.sum(got_ref[...], axis=0)
    v_ref[...] = v
    emit(1)
    alpha = v[EXT : EXT + 1] / v[EXT + 1 : EXT + 2]
    u0 = u_ref[...]
    u1 = u0 - alpha * v
    packed = pack(v)
    wt = w_ref[...].T
    rows = []
    rz = jnp.zeros((8, BLK), F32)
    zaz = jnp.zeros((8, BLK), F32)
    cross = jnp.zeros((8, BLK), F32)
    for c, blocks in chunks():
        ready(c)
        for i in blocks:
            col = wt[:, i : i + 1]
            image = im_ref[i]
            dr = dr_ref[i]
            z0 = dr + col * u0[i : i + 1]
            z1 = dr - alpha * dim_ref[i] + col * u1[i : i + 1]
            az = image - alpha * (adim_ref[i] + dot(q_ref[i], packed))
            rows.append(jnp.sum(col * az, axis=0, keepdims=True))
            rz = rz + fold((r_ref[i] - alpha * image) * z1)
            zaz = zaz + fold(z1 * az)
            cross = cross + fold(z1 * image + z0 * az)
    broadcast(msg_ref, message(rows, [rz, zaz, cross]))
    emit(0)


def last_body(
    ready, emit, got_ref, u_ref, v_ref, w_ref, r_ref, im_ref, dr_ref, dim_ref, az_ref, daz_ref,
    sol_ref, res_ref, pre_ref,
):
    t = jnp.sum(got_ref[...], axis=0)
    v = v_ref[...]
    gamma0 = v[EXT : EXT + 1]
    curve0 = v[EXT + 1 : EXT + 2]
    gamma1 = t[EXT : EXT + 1]
    alpha0 = gamma0 / curve0
    beta = gamma1 / gamma0
    curve1 = t[EXT + 1 : EXT + 2] + beta * (t[EXT + 2 : EXT + 3] + beta * curve0)
    alpha1 = gamma1 / curve1
    u0 = u_ref[...]
    u1 = u0 - alpha0 * v
    u2 = u1 - alpha1 * (t + beta * v)
    wt = w_ref[...].T
    for c, blocks in chunks():
        ready(c)
        for i in blocks:
            col = wt[:, i : i + 1]
            image = im_ref[i]
            dr = dr_ref[i]
            dim = dim_ref[i]
            z0 = dr + col * u0[i : i + 1]
            dr1 = dr - alpha0 * dim
            z1 = dr1 + col * u1[i : i + 1]
            sol_ref[i] = alpha0 * z0 + alpha1 * (z1 + beta * z0)
            res_ref[i] = r_ref[i] - alpha0 * image - alpha1 * (az_ref[i] + beta * image)
            local = dr1 - alpha1 * (daz_ref[i] + beta * dim)
            pre_ref[i] = local + col * u2[i : i + 1]
        for n in range(3):
            emit(n, c)


FIELD = (NB, BLK, BLK)


def apply_operator(stiffness, columns, field, inner, outer, weights=None):
    first = weights is not None
    hbm = pl.BlockSpec(memory_space=pltpu.HBM)
    outs = [jax.ShapeDtypeStruct(FIELD, F32)]
    args = [columns, stiffness, field, inner, outer]
    scratch = [
        pltpu.SMEM(columns.shape, jnp.int32),
        pltpu.VMEM(stiffness.shape, F32),
        pltpu.VMEM(FIELD, F32),
        pltpu.VMEM(inner.shape, F32),
        pltpu.VMEM(outer.shape, F32),
        pltpu.VMEM(FIELD, F32),
        pltpu.VMEM((EXT, BLK, 2 * BLK), BF16),
        pltpu.SemaphoreType.DMA((NB // GROUP + 5,)),
        pltpu.SemaphoreType.DMA((2, NB // GROUP)),
    ]
    if first:
        outs.append(jax.ShapeDtypeStruct(FIELD, BF16))
        args.append(weights)
        scratch += [
            pltpu.VMEM(weights.shape, F32),
            pltpu.VMEM(FIELD, BF16),
            pltpu.VMEM((EXT, BLK, 2 * BLK), BF16),
        ]
    return pl.pallas_call(
        functools.partial(operator_kernel, first),
        out_shape=outs,
        in_specs=[hbm] * 3 + [pl.BlockSpec(memory_space=pl.ANY)] * 2 + [hbm] * (len(args) - 5),
        out_specs=[hbm] * len(outs),
        scratch_shapes=scratch,
        compiler_params=pltpu.CompilerParams(vmem_limit_bytes=BIG),
        cost_estimate=pl.CostEstimate(flops=6 * 10**9, bytes_accessed=8 << 20, transcendentals=0),
    )(*args)


def on_device(
    loads, stiffness, inv_diag, columns, send_lists, restrict_weights, coarse_map, coarse_diag
):
    devices = lax.axis_size(RING)
    gathered = lax.axis_size(GATHER)
    scattered = lax.axis_size(SCATTER)
    swaps = []
    for first in (0, 1):
        pairs = [((first + 2 * i) % devices, (first + 2 * i + 1) % devices) for i in range(devices // 2)]
        swaps.append(pairs + [(j, i) for i, j in pairs])
    send = (send_lists.reshape(1, 2), "scalar")
    cells = (coarse_map, "scalar")
    columns = columns.T
    weights = (restrict_weights, "whole")

    def msg_out(extra):
        return ((gathered, NB + extra, BLK), F32, "whole")

    part_shape = (scattered, ROWS, BLK)
    part_out = (part_shape, F32, "whole")
    short_out = (part_shape[1:], F32, "whole")
    field_out = (FIELD, F32, "field")
    big = 2 << 20

    (target,) = staged(
        target_body,
        [send, cells, (coarse_diag, "whole")],
        [((scattered, TROWS, BLK), F32, "whole")],
        moved=1 << 18,
    )
    targets = lax.all_to_all(target, SCATTER, 0, 0, tiled=True)
    (start_rows,) = staged(
        start_body,
        [cells, weights, (loads, "field")],
        [((ROWS, BLK), F32, "vmem")],
        flops=10**6,
        moved=big,
    )
    (msg,) = staged(
        open_body, [(start_rows, "vmem"), (targets, "vmem")], [msg_out(2)], moved=1 << 18, limit=SMALL
    )
    got = lax.all_to_all(msg, GATHER, 0, 0, tiled=True)
    packet = ((BLK + 8, BLK), F32, "vmem")
    local, inner, outer, local_dot = staged(
        local_body,
        [send, weights, (loads, "field"), (inv_diag, "field")],
        [field_out, packet, packet, ((8, BLK), F32, "whole")],
        flops=2 * 10**8,
        moved=big,
    )
    inner = lax.ppermute(inner, RING, swaps[0])
    outer = lax.ppermute(outer, RING, swaps[1])
    rows = scattered * EXT
    coarse_rows, coarse_inv = staged(
        sweep_body,
        [(targets, "vmem")],
        [((2 * rows, CROWS * BLK), BF16, "whole"), ((CROWS, BLK), F32, "whole")],
        scratch=[pltpu.VMEM((rows, BLK), F32), pltpu.VMEM((CROWS, rows, BLK), F32)],
        flops=10**8,
        moved=big,
        limit=SMALL,
    )
    got, inner = lax.optimization_barrier((got, inner))
    image_local, coupling = apply_operator(
        stiffness, columns, local, inner, outer, restrict_weights
    )
    weights_out = ((rows, gathered * NB), BF16, "whole")
    cells_all = CROWS * BLK
    part, wh, wl = staged(
        coarse_body,
        [(coarse_rows, "hbm"), (coarse_inv, "hbm"), (got, "vmem")],
        [part_out, weights_out, weights_out],
        scratch=[
            pltpu.VMEM((2 * rows, cells_all), BF16),
            pltpu.VMEM((CROWS, BLK), F32),
            pltpu.VMEM((cells_all, gathered * NB), BF16),
            pltpu.SemaphoreType.DMA((2,)),
        ],
        flops=10**9,
        moved=big,
        limit=SMALL,
    )
    got = lax.all_to_all(part, SCATTER, 0, 0, tiled=True)

    msg, u0 = staged(
        first_body,
        [(got, "any"), weights, (start_rows, "whole"), (local_dot, "whole"), (local, "field"),
         (image_local, "field"), (coupling, "field")],
        [msg_out(2), short_out],
        flops=10**8,
        moved=big,
    )
    packet = ((BLK, BLK), F32, "vmem")
    image0, local_image, inner, outer = staged(
        image_body,
        [send, (u0, "whole"), (image_local, "field"), (coupling, "field"), (inv_diag, "field")],
        [field_out, field_out, packet, packet],
        flops=2 * 10**8,
        moved=big,
    )
    inner = lax.ppermute(inner, RING, swaps[0])
    outer = lax.ppermute(outer, RING, swaps[1])
    (image_image,) = apply_operator(stiffness, columns, local_image, inner, outer)

    def exchange(got):
        (part,) = staged(
            apply_body,
            [(wh, "whole"), (wl, "whole"), (got, "vmem")],
            [part_out],
            flops=10**8,
            moved=big,
            limit=SMALL,
        )
        return lax.all_to_all(part, SCATTER, 0, 0, tiled=True)

    got = exchange(lax.all_to_all(msg, GATHER, 0, 0, tiled=True))
    msg, v0 = staged(
        second_body,
        [(got, "any"), (u0, "whole"), weights, (loads, "field"), (image0, "field"),
         (local, "field"), (local_image, "field"), (image_image, "field"),
         (coupling, "field")],
        [msg_out(3), short_out],
        flops=10**8,
        moved=big,
    )
    image1, local_image1 = staged(
        product_body,
        [(v0, "whole"), (image0, "field"), (image_image, "field"), (coupling, "field"),
         (inv_diag, "field")],
        [field_out] * 2,
        flops=2 * 10**8,
        moved=big,
    )
    got = lax.all_to_all(msg, GATHER, 0, 0, tiled=True)
    got, local_image1 = lax.optimization_barrier((got, local_image1))
    got = exchange(got)
    return tuple(
        staged(
            last_body,
            [(got, "any"), (u0, "whole"), (v0, "whole"), weights, (loads, "field"),
             (image0, "field"), (local, "field"), (local_image, "field"), (image1, "field"),
             (local_image1, "field")],
            [field_out] * 3,
            flops=10**8,
            moved=big,
        )
    )


def solution(mesh):
    chips = mesh.devices.reshape(4, 8, 2, mesh.shape["crs"])
    fine = Mesh(chips, RING)
    placed = P(RING)
    return jax.shard_map(
        on_device,
        mesh=fine,
        in_specs=(placed,) * 7 + (P(),),
        out_specs=(placed,) * 3,
        check_vma=False,
    )
```
